256 devices in a mesh: row: 16 (over y, z_lo), col: 16 (over z_hi, x, core).
Axes of the slice: x: 4, y: 4, z: 8 (z_hi: 2, z_lo: 4; z = z_hi * 4 + z_lo), core: 2. Of those that a mesh axis runs over, the one named last changes fastest.
Arguments:
- values: float32 [8192, 8192], P('row', 'col'), may hold values from 0.05 to 16
- tile_mask: int32 [32, 32], P('row', 'col'), may hold values from 0 to 1, as said below
Outputs:
- inflated: float32 [8192, 8192], P('row', 'col')
The draws below stay inside these ranges and needn't reach their ends.
Inputs may be any that keep to these rules, and one draw needn't show every extreme that they name: `tile_mask`: every diagonal tile is 1; other tiles are 1 with a probability that differs by tile row and tile column.
All inputs are finite; a program needn't handle non-finite values.
Results may differ from the reference program's by a relative error of at most 0.00033.
Values may be sent and summed in bfloat16 or wider, within the bound.
A program may use at most 64 MiB of HBM per device.

```python
import math
import jax
import jax.numpy as jnp

TILE = 256
NTILES = 32
NODES = 8192


def draw_values(key, part):
    key = jax.random.fold_in(key, 11)
    first, second = jax.random.split(key, 2)
    entries = jax.random.uniform(first, (NODES, NODES), jnp.float32, 0.1, 1.0)
    scales = jnp.exp(jax.random.uniform(second, (NODES, 1), jnp.float32, 0.0, math.log(10.0)))
    return jnp.clip(entries * scales, 0.05, 16.0)


def draw_tile_mask(key, part):
    key = jax.random.fold_in(key, 23)
    first, second, third = jax.random.split(key, 3)
    row_weight = jax.random.randint(first, (NTILES, 1), 1, 9)
    col_weight = jax.random.randint(second, (1, NTILES), 1, 9)
    ticket = jax.random.randint(third, (NTILES, NTILES), 0, 64)
    ones = (ticket < row_weight * col_weight).astype(jnp.int32)
    diagonal = (jnp.arange(NTILES)[:, None] == jnp.arange(NTILES)[None, :]).astype(jnp.int32)
    return jnp.maximum(ones, diagonal)


def setup_inputs(seed: int = 0) -> dict:
    keys = jax.random.split(jax.random.key(seed), 3)
    return {
        "values": draw_values(jax.random.fold_in(keys[2], 71), 0),
        "tile_mask": draw_tile_mask(jax.random.fold_in(keys[2], 71), 0),
    }


def reference(values, tile_mask):
    tile_ones = jnp.repeat(jnp.repeat(tile_mask, TILE, axis=0), TILE, axis=1).astype(jnp.float32)
    masked = values * tile_ones
    colsum = jnp.sum(masked, axis=0)
    stoch = (masked / colsum[None, :]).astype(jnp.bfloat16)
    expanded = jnp.dot(stoch, stoch, preferred_element_type=jnp.float32)
    squared = expanded * expanded
    column_total = jnp.sum(squared, axis=0)
    return jnp.float32(NODES) * squared / column_total[None, :]
```

```python
import jax
import jax.numpy as jnp
from jax import lax
from jax.experimental import pallas as pl
from jax.experimental.pallas import tpu as pltpu
from jax.sharding import PartitionSpec as P

TILE = 256
BLK = 512
HALF = BLK // 2
NBLK = 16
MESH = pl.DeviceIdType.MESH


def kernel(
    values_ref,
    mask_ref,
    c_ref,
    total_ref,
    a_buf,
    b_buf,
    masked,
    sums,
    send,
    z_recv,
    y_recv,
    x_recv,
    zh_recv,
    core_recv,
    sum_send,
    sum_recv,
):
    r = lax.axis_index("row")
    c = lax.axis_index("col")
    y, zl = r // 4, r % 4
    zh, x, core = c // 8, (c // 2) % 4, c % 2
    middle = (zl + 1) // 2 == 1
    near = zl + 1 - 2 * (zl % 2)
    far_side = 3 - zl
    order = [zl, near, 2 - zl // 2, 3 - 3 * (zl // 2)]

    def at_y(d):
        return (((y + d) % 4) * 4 + zl, c)

    def at_zl(z):
        return (y * 4 + z, c)

    def at_x(d):
        return (r, zh * 8 + ((x + d) % 4) * 2 + core)

    across = (r, (c + 8) % 16)
    sibling = (r, c + 1 - 2 * core)

    barrier = pltpu.get_barrier_semaphore()
    partners = [at_y(d) for d in (1, 2, 3)] + [at_zl((zl + d) % 4) for d in (1, 2, 3)]
    partners += [at_x(1), at_x(3), across, sibling]
    for p in partners:
        pl.semaphore_signal(barrier, inc=1, device_id=p, device_id_type=MESH)

    for i in range(2):
        for j in range(2):
            rows, cols = pl.ds(i * TILE, TILE), pl.ds(j * TILE, TILE)
            masked[rows, cols] = values_ref[rows, cols] * mask_ref[i, j].astype(jnp.float32)
    sums[0, y] = jnp.sum(masked[...], axis=0, keepdims=True)
    c_ref[...] = jnp.zeros_like(c_ref)
    pl.semaphore_wait(barrier, len(partners))

    def all_sum(base):
        for stage, me, peer in ((0, y, at_y), (1, zl, lambda d: at_zl((zl + d) % 4))):
            slot = base + stage
            if stage == 1:
                sums[slot, zl] = sums[base, 0] + sums[base, 1] + sums[base, 2] + sums[base, 3]
            copies = []
            for d in (1, 2, 3):
                cp = pltpu.make_async_remote_copy(
                    src_ref=sums.at[slot, me],
                    dst_ref=sums.at[slot, me],
                    send_sem=sum_send.at[slot, d - 1],
                    recv_sem=sum_recv.at[slot, d - 1],
                    device_id=peer(d),
                    device_id_type=MESH,
                )
                cp.start()
                copies.append(cp)
            for d, cp in zip((1, 2, 3), copies):
                src = (me + 4 - d) % 4
                pltpu.make_async_remote_copy(
                    src_ref=sums.at[slot, src],
                    dst_ref=sums.at[slot, src],
                    send_sem=sum_send.at[slot, d - 1],
                    recv_sem=sum_recv.at[slot, d - 1],
                    device_id=peer(d),
                    device_id_type=MESH,
                ).wait_recv()
            for cp in copies:
                cp.wait_send()
        slot = base + 1
        return sums[slot, 0] + sums[slot, 1] + sums[slot, 2] + sums[slot, 3]

    colsum = all_sum(0)
    stoch = (masked[...] / colsum).astype(jnp.bfloat16)
    a_buf[c] = stoch
    b_buf[r] = stoch

    pending = []

    def push(buf, k, h, sem, dev, cond=None):
        part = buf.at[k] if h is None else buf.at[k, pl.ds(h * HALF, HALF)]
        cp = pltpu.make_async_remote_copy(
            src_ref=part,
            dst_ref=part,
            send_sem=send.at[len(pending)],
            recv_sem=sem,
            device_id=dev,
            device_id_type=MESH,
        )
        if cond is None:
            cp.start()
        else:
            pl.when(cond)(cp.start)
        pending.append((cp, cond))

    def take(buf, k, h, sem):
        part = buf.at[k] if h is None else buf.at[k, pl.ds(h * HALF, HALF)]
        pltpu.make_async_remote_copy(
            src_ref=part,
            dst_ref=part,
            send_sem=send.at[0],
            recv_sem=sem,
            device_id=sibling,
            device_id_type=MESH,
        ).wait_recv()

    def b_row(d, q):
        return ((y + d) % 4) * 4 + order[q]

    def a_col(s, d):
        return ((zh + s) % 2) * 8 + ((x + d) % 4) * 2 + core

    def z_start(h):
        push(b_buf, r, h, z_recv.at[zl, h], at_zl(near))
        push(b_buf, r, h, z_recv.at[zl, h], at_zl(far_side), middle)

    def z_take(q, h):
        o = order[q]
        take(b_buf, y * 4 + o, h, z_recv.at[o, h])
        push(b_buf, y * 4 + o, h, z_recv.at[o, h], at_zl(far_side if q == 1 else near), middle)
        y_start(q, h)

    def y_start(q, h):
        k = b_row(0, q)
        push(b_buf, k, h, y_recv.at[0, q, h], at_y(1))
        push(b_buf, k, h, y_recv.at[1, q, h], at_y(3))

    def y_forward(q, h):
        k = b_row(3 if h == 0 else 1, q)
        take(b_buf, k, h, y_recv.at[h, q, h])
        push(b_buf, k, h, y_recv.at[2, q, h], at_y(1 if h == 0 else 3))

    def x_start(s, h):
        k = a_col(s, 0)
        push(a_buf, k, h, x_recv.at[s, 0, h], at_x(1))
        push(a_buf, k, h, x_recv.at[s, 1, h], at_x(3))

    def x_forward(s, h):
        k = a_col(s, 3 if h == 0 else 1)
        take(a_buf, k, h, x_recv.at[s, h, h])
        push(a_buf, k, h, x_recv.at[s, 2, h], at_x(1 if h == 0 else 3))

    def to_sibling(s, d):
        push(a_buf, a_col(s, d), None, core_recv.at[s, d], sibling)

    def x_share(s):
        take(a_buf, a_col(s, 3), 1, x_recv.at[s, 0, 1])
        to_sibling(s, 3)
        take(a_buf, a_col(s, 1), 0, x_recv.at[s, 1, 0])
        to_sibling(s, 1)

    def x_share_far(s):
        for h in (0, 1):
            take(a_buf, a_col(s, 2), h, x_recv.at[s, 2, h])
        to_sibling(s, 2)

    for h in (0, 1):
        z_start(h)
        y_start(0, h)
        x_start(0, h)
    for h in (0, 1):
        push(a_buf, c, h, zh_recv.at[h], across)
    to_sibling(0, 0)

    z_take(1, 0)
    y_forward(0, 0)
    x_forward(0, 0)
    z_take(1, 1)
    y_forward(0, 1)
    x_forward(0, 1)
    x_share(0)
    z_take(2, 0)
    y_forward(1, 0)
    z_take(2, 1)
    y_forward(1, 1)
    x_share_far(0)
    for h in (0, 1):
        take(a_buf, a_col(1, 0), h, zh_recv.at[h])
        x_start(1, h)
    to_sibling(1, 0)
    z_take(3, 0)
    y_forward(2, 0)
    z_take(3, 1)
    x_forward(1, 0)
    y_forward(2, 1)
    x_forward(1, 1)
    x_share(1)
    y_forward(3, 0)
    y_forward(3, 1)
    x_share_far(1)

    def other_half(q):
        take(b_buf, b_row(3, q), 1, y_recv.at[0, q, 1])
        take(b_buf, b_row(1, q), 0, y_recv.at[1, q, 0])

    def far(q):
        for h in (0, 1):
            take(b_buf, b_row(2, q), h, y_recv.at[2, q, h])

    for s in (0, 1):
        for d in range(4):
            k = ((zh + s) % 2) * 8 + ((x + d) % 4) * 2 + 1 - core
            take(a_buf, k, None, core_recv.at[s, d])

    def product(k):
        c_ref[...] += jnp.dot(a_buf[k], b_buf[k], preferred_element_type=jnp.float32)

    for q in range(3):
        other_half(q)
        far(q)

    @pl.loop(0, 12)
    def _(i):
        product((i // 3) * 4 + (order[3] + 1 + i % 3) % 4)

    other_half(3)

    @pl.loop(0, 3)
    def _(i):
        product(((y + 3 + i) % 4) * 4 + order[3])

    far(3)
    product(b_row(2, 3))

    sums[2, y] = jnp.sum(c_ref[...] * c_ref[...], axis=0, keepdims=True)
    total_ref[...] = all_sum(2)
    for cp, cond in pending:
        if cond is None:
            cp.wait_send()
        else:
            pl.when(cond)(cp.wait_send)


def shards(values, tile_mask):
    product, total = pl.pallas_call(
        kernel,
        out_shape=(
            jax.ShapeDtypeStruct((BLK, BLK), jnp.float32),
            jax.ShapeDtypeStruct((1, BLK), jnp.float32),
        ),
        in_specs=[
            pl.BlockSpec(memory_space=pltpu.VMEM),
            pl.BlockSpec(memory_space=pltpu.SMEM),
        ],
        out_specs=(
            pl.BlockSpec(memory_space=pltpu.VMEM),
            pl.BlockSpec(memory_space=pltpu.VMEM),
        ),
        scratch_shapes=[
            pltpu.VMEM((NBLK, BLK, BLK), jnp.bfloat16),
            pltpu.VMEM((NBLK, BLK, BLK), jnp.bfloat16),
            pltpu.VMEM((BLK, BLK), jnp.float32),
            pltpu.VMEM((4, 4, 1, BLK), jnp.float32),
            pltpu.SemaphoreType.DMA((80,)),
            pltpu.SemaphoreType.DMA((4, 2)),
            pltpu.SemaphoreType.DMA((3, 4, 2)),
            pltpu.SemaphoreType.DMA((2, 3, 2)),
            pltpu.SemaphoreType.DMA((2,)),
            pltpu.SemaphoreType.DMA((2, 4)),
            pltpu.SemaphoreType.DMA((4, 3)),
            pltpu.SemaphoreType.DMA((4, 3)),
        ],
        compiler_params=pltpu.CompilerParams(
            collective_id=0, has_side_effects=True, vmem_limit_bytes=48 * 2**20
        ),
        cost_estimate=pl.CostEstimate(
            flops=2 * BLK * BLK * BLK * NBLK, bytes_accessed=4 * 2**20, transcendentals=0
        ),
    )(values, tile_mask)
    return jnp.float32(BLK * NBLK) * (product * product) / total


def solution(mesh):
    return jax.shard_map(
        shards,
        mesh=mesh,
        in_specs=(P("row", "col"), P("row", "col")),
        out_specs=P("row", "col"),
        check_vma=False,
    )
```

```python
import jax
import jax.numpy as jnp
from jax import lax
from jax.experimental import pallas as pl
from jax.experimental.pallas import tpu as pltpu
from jax.sharding import PartitionSpec as P

TILE = 256
BLK = 512
HALF = BLK // 2
PARTS = 4
NBLK = 16
MESH = pl.DeviceIdType.MESH


def kernel(
    values_hbm,
    mask_hbm,
    c_ref,
    total_ref,
    a_buf,
    b_buf,
    masked,
    sums,
    send,
    z_recv,
    y_recv,
    x_recv,
    zh_recv,
    core_recv,
    sum_send,
    sum_recv,
    values_ref,
    mask_ref,
    in_sem,
):
    r = lax.axis_index("row")
    c = lax.axis_index("col")
    y, zl = r // 4, r % 4
    zh, x, core = c // 8, (c // 2) % 4, c % 2
    middle = (zl + 1) // 2 == 1
    near = zl + 1 - 2 * (zl % 2)
    far_side = 3 - zl
    order = [zl, near, 2 - zl // 2, 3 - 3 * (zl // 2)]

    def at_y(d):
        return (((y + d) % 4) * 4 + zl, c)

    def at_zl(z):
        return (y * 4 + z, c)

    def at_x(d):
        return (r, zh * 8 + ((x + d) % 4) * 2 + core)

    across = (r, (c + 8) % 16)
    sibling = (r, c + 1 - 2 * core)

    values_in = pltpu.make_async_copy(values_hbm, values_ref, in_sem.at[0])
    mask_in = pltpu.make_async_copy(mask_hbm, mask_ref, in_sem.at[1])
    values_in.start()
    mask_in.start()

    barrier = pltpu.get_barrier_semaphore()
    shifts = [(dy, dz) for dy in range(4) for dz in range(4) if dy or dz]

    def in_column(dy, dz):
        return (((y + dy) % 4) * 4 + (zl + dz) % 4, c)

    partners = [in_column(dy, dz) for dy, dz in shifts]
    partners += [at_x(1), at_x(3), across, sibling]
    for p in partners:
        pl.semaphore_signal(barrier, inc=1, device_id=p, device_id_type=MESH)

    mask_in.wait()
    values_in.wait()
    for i in range(2):
        for j in range(2):
            rows, cols = pl.ds(i * TILE, TILE), pl.ds(j * TILE, TILE)
            masked[rows, cols] = values_ref[rows, cols] * mask_ref[i, j].astype(jnp.float32)
    sums[0, r] = jnp.sum(masked[...], axis=0, keepdims=True)
    c_ref[...] = jnp.zeros_like(c_ref)
    pl.semaphore_wait(barrier, len(partners))

    def all_sum(base):
        copies = []
        for n, (dy, dz) in enumerate(shifts):
            cp = pltpu.make_async_remote_copy(
                src_ref=sums.at[base, r],
                dst_ref=sums.at[base, r],
                send_sem=sum_send.at[base, n],
                recv_sem=sum_recv.at[base, n],
                device_id=in_column(dy, dz),
                device_id_type=MESH,
            )
            cp.start()
            copies.append(cp)
        for n, (dy, dz) in enumerate(shifts):
            src = ((y + 4 - dy) % 4) * 4 + (zl + 4 - dz) % 4
            pltpu.make_async_remote_copy(
                src_ref=sums.at[base, src],
                dst_ref=sums.at[base, src],
                send_sem=sum_send.at[base, n],
                recv_sem=sum_recv.at[base, n],
                device_id=in_column(dy, dz),
                device_id_type=MESH,
            ).wait_recv()
        for cp in copies:
            cp.wait_send()
        return jnp.sum(sums[base], axis=0)

    colsum = all_sum(0)
    stoch = (masked[...] / colsum).astype(jnp.bfloat16)
    a_buf[c] = stoch
    b_buf[r] = stoch

    pending = []

    def piece(buf, k, h):
        if h is None:
            return buf.at[k]
        n = PARTS if buf is a_buf else 2
        return buf.at[k, pl.ds(h * (BLK // n), BLK // n)]


    def push(buf, k, h, sem, dev, cond=None):
        part = piece(buf, k, h)
        cp = pltpu.make_async_remote_copy(
            src_ref=part,
            dst_ref=part,
            send_sem=send.at[len(pending)],
            recv_sem=sem,
            device_id=dev,
            device_id_type=MESH,
        )
        if cond is None:
            cp.start()
        else:
            pl.when(cond)(cp.start)
        pending.append((cp, cond))

    def take(buf, k, h, sem):
        part = piece(buf, k, h)
        pltpu.make_async_remote_copy(
            src_ref=part,
            dst_ref=part,
            send_sem=send.at[0],
            recv_sem=sem,
            device_id=sibling,
            device_id_type=MESH,
        ).wait_recv()

    def b_row(d, q):
        return ((y + d) % 4) * 4 + order[q]

    def a_col(s, d):
        return ((zh + s) % 2) * 8 + ((x + d) % 4) * 2 + core

    def z_start(h):
        push(b_buf, r, h, z_recv.at[zl, h], at_zl(near))
        push(b_buf, r, h, z_recv.at[zl, h], at_zl(far_side), middle)

    def z_take(q, h):
        o = order[q]
        take(b_buf, y * 4 + o, h, z_recv.at[o, h])
        push(b_buf, y * 4 + o, h, z_recv.at[o, h], at_zl(far_side if q == 1 else near), middle)
        y_start(q, h)

    def y_start(q, h):
        k = b_row(0, q)
        push(b_buf, k, h, y_recv.at[0, q, h], at_y(1))
        push(b_buf, k, h, y_recv.at[1, q, h], at_y(3))

    def y_forward(q, h):
        k = b_row(3 if h == 0 else 1, q)
        take(b_buf, k, h, y_recv.at[h, q, h])
        push(b_buf, k, h, y_recv.at[2, q, h], at_y(1 if h == 0 else 3))

    def x_start(s, h):
        k = a_col(s, 0)
        push(a_buf, k, h, x_recv.at[s, 0, h], at_x(1))
        push(a_buf, k, h, x_recv.at[s, 1, h], at_x(3))

    def x_forward(s, h):
        d = 0 if h < PARTS // 2 else 1
        k = a_col(s, 3 if d == 0 else 1)
        take(a_buf, k, h, x_recv.at[s, d, h])
        push(a_buf, k, h, x_recv.at[s, 2, h], at_x(1 if d == 0 else 3))

    def to_sibling(s, d):
        push(a_buf, a_col(s, d), None, core_recv.at[s, d], sibling)

    def x_share(s):
        for h in range(PARTS // 2, PARTS):
            take(a_buf, a_col(s, 3), h, x_recv.at[s, 0, h])
        to_sibling(s, 3)
        for h in range(PARTS // 2):
            take(a_buf, a_col(s, 1), h, x_recv.at[s, 1, h])
        to_sibling(s, 1)

    def x_share_far(s):
        for h in range(PARTS):
            take(a_buf, a_col(s, 2), h, x_recv.at[s, 2, h])
        to_sibling(s, 2)

    def across_start(h):
        push(a_buf, c, h, zh_recv.at[h], across)

    def across_take(h):
        take(a_buf, a_col(1, 0), h, zh_recv.at[h])
        x_start(1, h)

    def rest(q):
        take(b_buf, b_row(3, q), 1, y_recv.at[0, q, 1])
        take(b_buf, b_row(1, q), 0, y_recv.at[1, q, 0])
        if q < 3:
            far(q)

    def far(q):
        for h in (0, 1):
            take(b_buf, b_row(2, q), h, y_recv.at[2, q, h])

    def from_sibling(s):
        for d in range(4):
            k = ((zh + s) % 2) * 8 + ((x + d) % 4) * 2 + 1 - core
            take(a_buf, k, None, core_recv.at[s, d])

    def product(k):
        c_ref[...] += jnp.dot(a_buf[k], b_buf[k], preferred_element_type=jnp.float32)

    def products(q, s):
        @pl.loop(0, 2)
        def _(i):
            product((((zh + s) % 2) * 2 + i) * 4 + order[q])

    def last():
        @pl.loop(0, 3)
        def _(i):
            product(((y + 3 + i) % 4) * 4 + order[3])

        far(3)
        product(b_row(2, 3))

    for h in (0, 1):
        z_start(h)
        y_start(0, h)
    x_start(0, 0)
    x_start(0, 1)
    x_start(0, 2)
    x_start(0, 3)
    to_sibling(0, 0)
    z_take(1, 0)
    y_forward(0, 0)
    x_forward(0, 0)
    x_forward(0, 1)
    z_take(1, 1)
    y_forward(0, 1)
    x_forward(0, 2)
    x_forward(0, 3)
    x_share(0)
    z_take(2, 0)
    y_forward(1, 0)
    across_start(0)
    z_take(2, 1)
    y_forward(1, 1)
    across_start(1)
    x_share_far(0)
    z_take(3, 0)
    y_forward(2, 0)
    across_start(2)
    z_take(3, 1)
    y_forward(2, 1)
    across_start(3)
    from_sibling(0)
    rest(0)
    products(0, 0)
    across_take(0)
    y_forward(3, 0)
    across_take(1)
    x_forward(1, 0)
    across_take(2)
    x_forward(1, 1)
    y_forward(3, 1)
    across_take(3)
    x_forward(1, 2)
    x_forward(1, 3)
    to_sibling(1, 0)
    rest(1)
    products(1, 0)
    rest(2)
    products(2, 0)
    x_share(1)
    x_share_far(1)
    from_sibling(1)
    products(0, 1)
    products(1, 1)
    products(2, 1)
    rest(3)
    last()

    sums[1, r] = jnp.sum(c_ref[...] * c_ref[...], axis=0, keepdims=True)
    total_ref[...] = all_sum(1)
    for cp, cond in pending:
        if cond is None:
            cp.wait_send()
        else:
            pl.when(cond)(cp.wait_send)


def shards(values, tile_mask):
    product, total = pl.pallas_call(
        kernel,
        out_shape=(
            jax.ShapeDtypeStruct((BLK, BLK), jnp.float32),
            jax.ShapeDtypeStruct((1, BLK), jnp.float32),
        ),
        in_specs=[
            pl.BlockSpec(memory_space=pl.ANY),
            pl.BlockSpec(memory_space=pl.ANY),
        ],
        out_specs=(
            pl.BlockSpec(memory_space=pltpu.VMEM),
            pl.BlockSpec(memory_space=pltpu.VMEM),
        ),
        scratch_shapes=[
            pltpu.VMEM((NBLK, BLK, BLK), jnp.bfloat16),
            pltpu.VMEM((NBLK, BLK, BLK), jnp.bfloat16),
            pltpu.VMEM((BLK, BLK), jnp.float32),
            pltpu.VMEM((2, NBLK, 1, BLK), jnp.float32),
            pltpu.SemaphoreType.DMA((100,)),
            pltpu.SemaphoreType.DMA((4, 2)),
            pltpu.SemaphoreType.DMA((3, 4, 2)),
            pltpu.SemaphoreType.DMA((2, 3, PARTS)),
            pltpu.SemaphoreType.DMA((PARTS,)),
            pltpu.SemaphoreType.DMA((2, 4)),
            pltpu.SemaphoreType.DMA((2, 15)),
            pltpu.SemaphoreType.DMA((2, 15)),
            pltpu.VMEM((BLK, BLK), jnp.float32),
            pltpu.SMEM((2, 2), jnp.int32),
            pltpu.SemaphoreType.DMA((2,)),
        ],
        compiler_params=pltpu.CompilerParams(
            collective_id=0, has_side_effects=True, vmem_limit_bytes=48 * 2**20
        ),
        cost_estimate=pl.CostEstimate(
            flops=2 * BLK * BLK * BLK * NBLK, bytes_accessed=4 * 2**20, transcendentals=0
        ),
    )(values, tile_mask)
    return jnp.float32(BLK * NBLK) * (product * product) / total


def solution(mesh):
    return jax.shard_map(
        shards,
        mesh=mesh,
        in_specs=(P("row", "col"), P("row", "col")),
        out_specs=P("row", "col"),
        check_vma=False,
    )
```

```python
import jax
import jax.numpy as jnp
from jax import lax
from jax.experimental import pallas as pl
from jax.experimental.pallas import tpu as pltpu
from jax.sharding import PartitionSpec as P

TILE = 256
BLK = 512
HALF = BLK // 2
PARTS = 4
NBLK = 16
MESH = pl.DeviceIdType.MESH


def kernel(
    values_hbm,
    mask_hbm,
    c_ref,
    total_ref,
    a_buf,
    b_buf,
    masked,
    sums,
    send,
    z_recv,
    y_recv,
    x_recv,
    zh_recv,
    core_recv,
    far_recv,
    sum_send,
    sum_recv,
    values_ref,
    mask_ref,
    in_sem,
):
    r = lax.axis_index("row")
    c = lax.axis_index("col")
    y, zl = r // 4, r % 4
    zh, x, core = c // 8, (c // 2) % 4, c % 2
    middle = (zl + 1) // 2 == 1
    near = zl + 1 - 2 * (zl % 2)
    far_side = 3 - zl
    order = [zl, near, 2 - zl // 2, 3 - 3 * (zl // 2)]

    def at_y(d):
        return (((y + d) % 4) * 4 + zl, c)

    def at_zl(z):
        return (y * 4 + z, c)

    def at_x(d):
        return (r, zh * 8 + ((x + d) % 4) * 2 + core)

    across = (r, (c + 8) % 16)
    sibling = (r, c + 1 - 2 * core)

    values_in = pltpu.make_async_copy(values_hbm, values_ref, in_sem.at[0])
    mask_in = pltpu.make_async_copy(mask_hbm, mask_ref, in_sem.at[1])
    values_in.start()
    mask_in.start()

    barrier = pltpu.get_barrier_semaphore()
    shifts = [(dy, dz) for dy in range(4) for dz in range(4) if dy or dz]

    def in_column(dy, dz):
        return (((y + dy) % 4) * 4 + (zl + dz) % 4, c)

    partners = [in_column(dy, dz) for dy, dz in shifts]
    partners += [at_x(1), at_x(3), across, sibling]
    for p in partners:
        pl.semaphore_signal(barrier, inc=1, device_id=p, device_id_type=MESH)

    mask_in.wait()
    values_in.wait()
    for i in range(2):
        for j in range(2):
            rows, cols = pl.ds(i * TILE, TILE), pl.ds(j * TILE, TILE)
            masked[rows, cols] = values_ref[rows, cols] * mask_ref[i, j].astype(jnp.float32)
    sums[0, r] = jnp.sum(masked[...], axis=0, keepdims=True)
    c_ref[...] = jnp.zeros_like(c_ref)
    pl.semaphore_wait(barrier, len(partners))

    def all_sum(base):
        copies = []
        for n, (dy, dz) in enumerate(shifts):
            cp = pltpu.make_async_remote_copy(
                src_ref=sums.at[base, r],
                dst_ref=sums.at[base, r],
                send_sem=sum_send.at[base, n],
                recv_sem=sum_recv.at[base, n],
                device_id=in_column(dy, dz),
                device_id_type=MESH,
            )
            cp.start()
            copies.append(cp)
        for n, (dy, dz) in enumerate(shifts):
            src = ((y + 4 - dy) % 4) * 4 + (zl + 4 - dz) % 4
            pltpu.make_async_remote_copy(
                src_ref=sums.at[base, src],
                dst_ref=sums.at[base, src],
                send_sem=sum_send.at[base, n],
                recv_sem=sum_recv.at[base, n],
                device_id=in_column(dy, dz),
                device_id_type=MESH,
            ).wait_recv()
        for cp in copies:
            cp.wait_send()
        return jnp.sum(sums[base], axis=0)

    colsum = all_sum(0)
    stoch = (masked[...] / colsum).astype(jnp.bfloat16)
    a_buf[c] = stoch
    b_buf[r] = stoch

    pending = []
    inner = []

    def piece(buf, k, h):
        if h is None:
            return buf.at[k]
        n = PARTS if buf is a_buf else 2
        return buf.at[k, pl.ds(h * (BLK // n), BLK // n)]


    def push(buf, k, h, sem, dev):
        part = piece(buf, k, h)
        cp = pltpu.make_async_remote_copy(
            src_ref=part,
            dst_ref=part,
            send_sem=send.at[len(pending)],
            recv_sem=sem,
            device_id=dev,
            device_id_type=MESH,
        )
        cp.start()
        pending.append(cp)

    def take(buf, k, h, sem):
        part = piece(buf, k, h)
        pltpu.make_async_remote_copy(
            src_ref=part,
            dst_ref=part,
            send_sem=send.at[0],
            recv_sem=sem,
            device_id=sibling,
            device_id_type=MESH,
        ).wait_recv()

    def b_row(d, q):
        return ((y + d) % 4) * 4 + order[q]

    def a_col(s, d):
        return ((zh + s) % 2) * 8 + ((x + d) % 4) * 2 + core

    def z_start(h):
        push(b_buf, r, h, z_recv.at[zl, h], at_zl(near))
        if inner[-1]:
            push(b_buf, r, h, z_recv.at[zl, h], at_zl(far_side))

    def z_take(q, h):
        o = order[q]
        take(b_buf, y * 4 + o, h, z_recv.at[o, h])
        if inner[-1]:
            push(b_buf, y * 4 + o, h, z_recv.at[o, h], at_zl(far_side if q == 1 else near))
        y_start(q, h)

    def y_start(q, h):
        k = b_row(0, q)
        push(b_buf, k, h, y_recv.at[0, q, h], at_y(1))
        push(b_buf, k, h, y_recv.at[1, q, h], at_y(3))

    def y_forward(q, h):
        k = b_row(3 if h == 0 else 1, q)
        take(b_buf, k, h, y_recv.at[h, q, h])
        push(b_buf, k, h, y_recv.at[2, q, h], at_y(1 if h == 0 else 3))

    def x_start(s, h):
        k = a_col(s, 0)
        push(a_buf, k, h, x_recv.at[s, 0, h], at_x(1))
        push(a_buf, k, h, x_recv.at[s, 1, h], at_x(3))

    def x_forward(s, h):
        d = 0 if h < PARTS // 2 else 1
        k = a_col(s, 3 if d == 0 else 1)
        take(a_buf, k, h, x_recv.at[s, d, h])
        push(a_buf, k, h, x_recv.at[s, 2, h], at_x(1 if d == 0 else 3))

    def to_sibling(s, d):
        push(a_buf, a_col(s, d), None, core_recv.at[s, d], sibling)

    def x_share(s):
        for h in range(PARTS // 2, PARTS):
            take(a_buf, a_col(s, 3), h, x_recv.at[s, 0, h])
        to_sibling(s, 3)
        for h in range(PARTS // 2):
            take(a_buf, a_col(s, 1), h, x_recv.at[s, 1, h])
        to_sibling(s, 1)

    def x_share_far(s):
        for h in range(PARTS):
            take(a_buf, a_col(s, 2), h, x_recv.at[s, 2, h])
            push(a_buf, a_col(s, 2), h, far_recv.at[s, h], sibling)

    def across_start(h):
        push(a_buf, c, h, zh_recv.at[h], across)

    def across_take(h):
        take(a_buf, a_col(1, 0), h, zh_recv.at[h])
        x_start(1, h)

    def rest(q):
        take(b_buf, b_row(3, q), 1, y_recv.at[0, q, 1])
        take(b_buf, b_row(1, q), 0, y_recv.at[1, q, 0])
        if q < 3:
            far(q)

    def far(q):
        for h in (0, 1):
            take(b_buf, b_row(2, q), h, y_recv.at[2, q, h])

    def from_sibling(s, d):
        k = ((zh + s) % 2) * 8 + ((x + d) % 4) * 2 + 1 - core
        if d == 2:
            for h in range(PARTS):
                take(a_buf, k, h, far_recv.at[s, h])
        else:
            take(a_buf, k, None, core_recv.at[s, d])

    def product(*ks):
        total = c_ref[...]
        for k in ks:
            total += jnp.dot(a_buf[k], b_buf[k], preferred_element_type=jnp.float32)
        c_ref[...] = total

    def products(q, s):
        k = ((zh + s) % 2) * 8 + order[q]
        product(k, k + 4)

    def sweep(stage):
        @pl.loop(0, NBLK)
        def _(k):
            a_late = jnp.where(k // 8 == zh, 0, jnp.where((k % 8) // 2 == (x + 2) % 4, 2, 1))
            b_late = jnp.where(k % 4 != order[3], 0, jnp.where(k // 4 == (y + 2) % 4, 2, 1))
            if stage == 0:
                now = (a_late == 1) & (b_late == 0)
            elif stage == 1:
                now = (a_late < 2) & (b_late == 1)
            else:
                now = (a_late == 2) | (b_late == 2)

            @pl.when(now)
            def _():
                product(k)

    def wait_sent():
        for cp in pending:
            cp.wait_send()

    @pl.when(jnp.logical_not(middle))
    def _():
        inner.append(False)
        pending.clear()
        z_start(0)
        z_start(1)
        y_start(0, 0)
        y_start(0, 1)
        x_start(0, 0)
        x_start(0, 1)
        x_start(0, 2)
        x_start(0, 3)
        to_sibling(0, 0)
        z_take(1, 0)
        y_forward(0, 0)
        across_start(0)
        y_forward(0, 1)
        x_forward(0, 0)
        x_forward(0, 1)
        x_forward(0, 2)
        x_forward(0, 3)
        z_take(1, 1)
        across_start(1)
        y_forward(1, 0)
        x_share(0)
        z_take(2, 0)
        across_start(2)
        y_forward(1, 1)
        across_start(3)
        x_share_far(0)
        z_take(2, 1)
        across_take(0)
        y_forward(2, 0)
        across_take(1)
        z_take(3, 0)
        across_take(2)
        y_forward(2, 1)
        across_take(3)
        z_take(3, 1)
        x_forward(1, 0)
        x_forward(1, 1)
        x_forward(1, 2)
        x_forward(1, 3)
        to_sibling(1, 0)
        from_sibling(0, 0)
        from_sibling(0, 3)
        from_sibling(0, 1)
        from_sibling(0, 2)
        rest(0)
        products(0, 0)
        rest(1)
        products(1, 0)
        y_forward(3, 0)
        x_share(1)
        y_forward(3, 1)
        x_share_far(1)
        rest(2)
        products(2, 0)
        from_sibling(1, 0)
        from_sibling(1, 3)
        from_sibling(1, 1)
        sweep(0)
        rest(3)
        sweep(1)
        from_sibling(1, 2)
        far(3)
        sweep(2)
        wait_sent()

    @pl.when(middle)
    def _():
        inner.append(True)
        pending.clear()
        z_start(0)
        z_start(1)
        y_start(0, 0)
        y_start(0, 1)
        x_start(0, 0)
        x_start(0, 1)
        x_start(0, 2)
        x_start(0, 3)
        to_sibling(0, 0)
        z_take(1, 0)
        z_take(2, 0)
        y_forward(0, 0)
        across_start(0)
        z_take(1, 1)
        z_take(2, 1)
        y_forward(0, 1)
        x_forward(0, 0)
        x_forward(0, 1)
        x_forward(0, 2)
        x_forward(0, 3)
        across_start(1)
        z_take(3, 0)
        y_forward(1, 0)
        x_share(0)
        z_take(3, 1)
        across_start(2)
        y_forward(1, 1)
        across_start(3)
        x_share_far(0)
        across_take(0)
        y_forward(2, 0)
        across_take(1)
        across_take(2)
        y_forward(2, 1)
        across_take(3)
        x_forward(1, 0)
        x_forward(1, 1)
        x_forward(1, 2)
        x_forward(1, 3)
        to_sibling(1, 0)
        from_sibling(0, 0)
        from_sibling(0, 3)
        from_sibling(0, 1)
        from_sibling(0, 2)
        rest(0)
        products(0, 0)
        rest(1)
        products(1, 0)
        y_forward(3, 0)
        x_share(1)
        y_forward(3, 1)
        x_share_far(1)
        rest(2)
        products(2, 0)
        from_sibling(1, 0)
        from_sibling(1, 3)
        from_sibling(1, 1)
        sweep(0)
        rest(3)
        sweep(1)
        from_sibling(1, 2)
        far(3)
        sweep(2)
        wait_sent()

    sums[1, r] = jnp.sum(c_ref[...] * c_ref[...], axis=0, keepdims=True)
    total_ref[...] = all_sum(1)


def shards(values, tile_mask):
    product, total = pl.pallas_call(
        kernel,
        out_shape=(
            jax.ShapeDtypeStruct((BLK, BLK), jnp.float32),
            jax.ShapeDtypeStruct((1, BLK), jnp.float32),
        ),
        in_specs=[
            pl.BlockSpec(memory_space=pltpu.HBM),
            pl.BlockSpec(memory_space=pltpu.HBM),
        ],
        out_specs=(
            pl.BlockSpec(memory_space=pltpu.VMEM),
            pl.BlockSpec(memory_space=pltpu.VMEM),
        ),
        scratch_shapes=[
            pltpu.VMEM((NBLK, BLK, BLK), jnp.bfloat16),
            pltpu.VMEM((NBLK, BLK, BLK), jnp.bfloat16),
            pltpu.VMEM((BLK, BLK), jnp.float32),
            pltpu.VMEM((2, NBLK, 1, BLK), jnp.float32),
            pltpu.SemaphoreType.DMA((110,)),
            pltpu.SemaphoreType.DMA((4, 2)),
            pltpu.SemaphoreType.DMA((3, 4, 2)),
            pltpu.SemaphoreType.DMA((2, 3, PARTS)),
            pltpu.SemaphoreType.DMA((PARTS,)),
            pltpu.SemaphoreType.DMA((2, 4)),
            pltpu.SemaphoreType.DMA((2, PARTS)),
            pltpu.SemaphoreType.DMA((2, 15)),
            pltpu.SemaphoreType.DMA((2, 15)),
            pltpu.VMEM((BLK, BLK), jnp.float32),
            pltpu.SMEM((2, 2), jnp.int32),
            pltpu.SemaphoreType.DMA((2,)),
        ],
        compiler_params=pltpu.CompilerParams(
            collective_id=0, has_side_effects=True, vmem_limit_bytes=48 * 2**20
        ),
        cost_estimate=pl.CostEstimate(
            flops=2 * BLK * BLK * BLK * NBLK, bytes_accessed=4 * 2**20, transcendentals=0
        ),
    )(values, tile_mask)
    return jnp.float32(BLK * NBLK) * (product * product) / total


def solution(mesh):
    return jax.shard_map(
        shards,
        mesh=mesh,
        in_specs=(P("row", "col"), P("row", "col")),
        out_specs=P("row", "col"),
        check_vma=False,
    )
```

```python
import jax
import jax.numpy as jnp
from jax import lax
from jax.experimental import pallas as pl
from jax.experimental.pallas import tpu as pltpu
from jax.sharding import PartitionSpec as P

TILE = 256
BLK = 512
HALF = BLK // 2
PARTS = 4
NBLK = 16
MESH = pl.DeviceIdType.MESH


def kernel(
    values_hbm,
    mask_hbm,
    scaled_ref,
    c_ref,
    a_buf,
    b_buf,
    masked,
    sums,
    send,
    z_recv,
    y_recv,
    x_recv,
    zh_recv,
    core_recv,
    far_recv,
    sum_send,
    sum_recv,
    values_ref,
    mask_ref,
    in_sem,
):
    r = lax.axis_index("row")
    c = lax.axis_index("col")
    y, zl = r // 4, r % 4
    zh, x, core = c // 8, (c // 2) % 4, c % 2
    middle = (zl + 1) // 2 == 1
    near = zl + 1 - 2 * (zl % 2)
    far_side = 3 - zl
    order = [zl, near, 2 - zl // 2, 3 - 3 * (zl // 2)]

    def at_y(d):
        return (((y + d) % 4) * 4 + zl, c)

    def at_zl(z):
        return (y * 4 + z, c)

    def at_x(d):
        return (r, zh * 8 + ((x + d) % 4) * 2 + core)

    across = (r, (c + 8) % 16)
    sibling = (r, c + 1 - 2 * core)

    values_in = pltpu.make_async_copy(values_hbm, values_ref, in_sem.at[0])
    mask_in = pltpu.make_async_copy(mask_hbm, mask_ref, in_sem.at[1])
    values_in.start()
    mask_in.start()

    barrier = pltpu.get_barrier_semaphore()
    shifts = [(dy, dz) for dy in range(4) for dz in range(4) if dy or dz]

    def in_column(dy, dz):
        return (((y + dy) % 4) * 4 + (zl + dz) % 4, c)

    partners = [in_column(dy, dz) for dy, dz in shifts]
    partners += [at_x(1), at_x(3), across, sibling]
    for p in partners:
        pl.semaphore_signal(barrier, inc=1, device_id=p, device_id_type=MESH)

    mask_in.wait()
    values_in.wait()
    for i in range(2):
        for j in range(2):
            rows, cols = pl.ds(i * TILE, TILE), pl.ds(j * TILE, TILE)
            masked[rows, cols] = values_ref[rows, cols] * mask_ref[i, j].astype(jnp.float32)
    sums[0, r] = jnp.sum(masked[...], axis=0, keepdims=True)
    pl.semaphore_wait(barrier, len(partners))

    def sum_copy(base, n, slot):
        return pltpu.make_async_remote_copy(
            src_ref=sums.at[base, slot],
            dst_ref=sums.at[base, slot],
            send_sem=sum_send.at[base, n],
            recv_sem=sum_recv.at[base, n],
            device_id=in_column(*shifts[n]),
            device_id_type=MESH,
        )

    def start_sum(base):
        for n in range(len(shifts)):
            sum_copy(base, n, r).start()

    def finish_sum(base):
        for n, (dy, dz) in enumerate(shifts):
            sum_copy(base, n, ((y + 4 - dy) % 4) * 4 + (zl + 4 - dz) % 4).wait_recv()
        for n in range(len(shifts)):
            sum_copy(base, n, r).wait_send()
        return jnp.sum(sums[base], axis=0)

    start_sum(0)
    c_ref[...] = jnp.zeros_like(c_ref)
    inverse = 1.0 / finish_sum(0)

    def make_stoch(h):
        rows = pl.ds(h * HALF, HALF)
        stoch = (masked[rows] * inverse).astype(jnp.bfloat16)
        b_buf[r, rows] = stoch
        a_buf[c, rows] = stoch


    pending = []
    inner = []

    def piece(buf, k, h):
        if h is None:
            return buf.at[k]
        n = PARTS if buf is a_buf else 2
        return buf.at[k, pl.ds(h * (BLK // n), BLK // n)]


    def push(buf, k, h, sem, dev):
        part = piece(buf, k, h)
        cp = pltpu.make_async_remote_copy(
            src_ref=part,
            dst_ref=part,
            send_sem=send.at[len(pending)],
            recv_sem=sem,
            device_id=dev,
            device_id_type=MESH,
        )
        cp.start()
        pending.append(cp)

    def take(buf, k, h, sem):
        part = piece(buf, k, h)
        pltpu.make_async_remote_copy(
            src_ref=part,
            dst_ref=part,
            send_sem=send.at[0],
            recv_sem=sem,
            device_id=sibling,
            device_id_type=MESH,
        ).wait_recv()

    def b_row(d, q):
        return ((y + d) % 4) * 4 + order[q]

    def a_col(s, d):
        return ((zh + s) % 2) * 8 + ((x + d) % 4) * 2 + core

    def z_start(h):
        push(b_buf, r, h, z_recv.at[zl, h], at_zl(near))
        if inner[-1]:
            push(b_buf, r, h, z_recv.at[zl, h], at_zl(far_side))

    def z_take(q, h):
        o = order[q]
        k = y * 4 + o
        take(b_buf, k, h, z_recv.at[o, h])
        if inner[-1]:
            push(b_buf, k, h, z_recv.at[o, h], at_zl(far_side if q == 1 else near))
        y_start(q, h)

    def y_start(q, h):
        k = b_row(0, q)
        push(b_buf, k, h, y_recv.at[0, q, h], at_y(1))
        push(b_buf, k, h, y_recv.at[1, q, h], at_y(3))

    def y_forward(q, h):
        k = b_row(3 if h == 0 else 1, q)
        take(b_buf, k, h, y_recv.at[h, q, h])
        push(b_buf, k, h, y_recv.at[2, q, h], at_y(1 if h == 0 else 3))

    def x_start(s, h):
        k = a_col(s, 0)
        push(a_buf, k, h, x_recv.at[s, 0, h], at_x(1))
        push(a_buf, k, h, x_recv.at[s, 1, h], at_x(3))

    def x_forward(s, h):
        d = 0 if h < PARTS // 2 else 1
        k = a_col(s, 3 if d == 0 else 1)
        take(a_buf, k, h, x_recv.at[s, d, h])
        push(a_buf, k, h, x_recv.at[s, 2, h], at_x(1 if d == 0 else 3))

    def to_sibling(s, d):
        push(a_buf, a_col(s, d), None, core_recv.at[s, d], sibling)

    def x_share(s):
        for h in range(PARTS // 2, PARTS):
            take(a_buf, a_col(s, 3), h, x_recv.at[s, 0, h])
        to_sibling(s, 3)
        for h in range(PARTS // 2):
            take(a_buf, a_col(s, 1), h, x_recv.at[s, 1, h])
        to_sibling(s, 1)

    def x_share_far(s):
        for h in range(PARTS):
            take(a_buf, a_col(s, 2), h, x_recv.at[s, 2, h])
            push(a_buf, a_col(s, 2), h, far_recv.at[s, h], sibling)

    def across_start(h):
        push(a_buf, c, h, zh_recv.at[h], across)

    def across_take(h):
        take(a_buf, a_col(1, 0), h, zh_recv.at[h])
        x_start(1, h)

    def rest(q):
        take(b_buf, b_row(3, q), 1, y_recv.at[0, q, 1])
        take(b_buf, b_row(1, q), 0, y_recv.at[1, q, 0])
        if q < 3:
            far(q)

    def far(q):
        for h in (0, 1):
            take(b_buf, b_row(2, q), h, y_recv.at[2, q, h])

    def from_sibling(s, d):
        k = ((zh + s) % 2) * 8 + ((x + d) % 4) * 2 + 1 - core
        if d == 2:
            for h in range(PARTS):
                take(a_buf, k, h, far_recv.at[s, h])
        else:
            take(a_buf, k, None, core_recv.at[s, d])

    def product(*ks):
        total = c_ref[...]
        for k in ks:
            total += jnp.dot(a_buf[k], b_buf[k], preferred_element_type=jnp.float32)
        c_ref[...] = total

    def products(q, s):
        k = ((zh + s) % 2) * 8 + order[q]
        product(k, k + 4)

    def a_late(k):
        return (k // 8 != zh) & ((k % 8) // 2 == (x + 2) % 4)

    def sweep_near():
        @pl.loop(0, NBLK // 2)
        def _(i):
            k = ((zh + 1) % 2) * 8 + i

            @pl.when(jnp.logical_not(a_late(k)) & (k % 4 != order[3]))
            def _():
                product(k)

    def sweep_fourth():
        for d in (0, 1, 3):
            k = b_row(d, 3)

            @pl.when(jnp.logical_not(a_late(k)))
            def _():
                product(k)

    def sweep_last():
        k = ((zh + 1) % 2) * 8 + ((x + 2) % 4) * 2
        product(k, k + 1)
        k = b_row(2, 3)

        @pl.when(jnp.logical_not(a_late(k)))
        def _():
            product(k)

    def wait_sent():
        for cp in pending:
            cp.wait_send()

    @pl.when(jnp.logical_not(middle))
    def _():
        inner.append(False)
        pending.clear()
        make_stoch(0)
        z_start(0)
        y_start(0, 0)
        make_stoch(1)
        z_start(1)
        y_start(0, 1)
        x_start(0, 0)
        x_start(0, 1)
        x_start(0, 2)
        x_start(0, 3)
        to_sibling(0, 0)
        z_take(1, 0)
        y_forward(0, 0)
        across_start(0)
        y_forward(0, 1)
        x_forward(0, 0)
        x_forward(0, 1)
        x_forward(0, 2)
        x_forward(0, 3)
        z_take(1, 1)
        across_start(1)
        y_forward(1, 0)
        x_share(0)
        z_take(2, 0)
        across_start(2)
        y_forward(1, 1)
        across_start(3)
        x_share_far(0)
        from_sibling(0, 0)
        from_sibling(0, 3)
        from_sibling(0, 1)
        from_sibling(0, 2)
        rest(0)
        products(0, 0)
        z_take(2, 1)
        across_take(0)
        y_forward(2, 0)
        across_take(1)
        z_take(3, 0)
        across_take(2)
        y_forward(2, 1)
        across_take(3)
        x_forward(1, 0)
        x_forward(1, 1)
        rest(1)
        products(1, 0)
        z_take(3, 1)
        x_forward(1, 2)
        x_forward(1, 3)
        to_sibling(1, 0)
        y_forward(3, 0)
        x_share(1)
        y_forward(3, 1)
        x_share_far(1)
        rest(2)
        products(2, 0)
        from_sibling(1, 0)
        from_sibling(1, 3)
        from_sibling(1, 1)
        sweep_near()
        rest(3)
        sweep_fourth()
        far(3)
        from_sibling(1, 2)
        sweep_last()
        wait_sent()

    @pl.when(middle)
    def _():
        inner.append(True)
        pending.clear()
        make_stoch(0)
        z_start(0)
        y_start(0, 0)
        make_stoch(1)
        z_start(1)
        y_start(0, 1)
        x_start(0, 0)
        x_start(0, 1)
        x_start(0, 2)
        x_start(0, 3)
        to_sibling(0, 0)
        z_take(1, 0)
        z_take(2, 0)
        y_forward(0, 0)
        across_start(0)
        z_take(1, 1)
        z_take(2, 1)
        y_forward(0, 1)
        x_forward(0, 0)
        x_forward(0, 1)
        x_forward(0, 2)
        x_forward(0, 3)
        across_start(1)
        z_take(3, 0)
        y_forward(1, 0)
        x_share(0)
        z_take(3, 1)
        across_start(2)
        y_forward(1, 1)
        across_start(3)
        x_share_far(0)
        from_sibling(0, 0)
        from_sibling(0, 3)
        from_sibling(0, 1)
        from_sibling(0, 2)
        rest(0)
        products(0, 0)
        across_take(0)
        y_forward(2, 0)
        across_take(1)
        across_take(2)
        y_forward(2, 1)
        across_take(3)
        rest(1)
        products(1, 0)
        x_forward(1, 0)
        x_forward(1, 1)
        x_forward(1, 2)
        x_forward(1, 3)
        to_sibling(1, 0)
        y_forward(3, 0)
        x_share(1)
        y_forward(3, 1)
        x_share_far(1)
        rest(2)
        products(2, 0)
        from_sibling(1, 0)
        from_sibling(1, 3)
        from_sibling(1, 1)
        sweep_near()
        rest(3)
        sweep_fourth()
        far(3)
        from_sibling(1, 2)
        sweep_last()
        wait_sent()

    sums[1, r] = jnp.sum(c_ref[...] * c_ref[...], axis=0, keepdims=True)
    start_sum(1)
    scaled_ref[...] = c_ref[...] * jnp.sqrt(jnp.float32(BLK * NBLK) / finish_sum(1))


def shards(values, tile_mask):
    scaled = pl.pallas_call(
        kernel,
        out_shape=jax.ShapeDtypeStruct((BLK, BLK), jnp.float32),
        in_specs=[
            pl.BlockSpec(memory_space=pltpu.HBM),
            pl.BlockSpec(memory_space=pltpu.HBM),
        ],
        out_specs=pl.BlockSpec(memory_space=pltpu.VMEM),
        scratch_shapes=[
            pltpu.VMEM((BLK, BLK), jnp.float32),
            pltpu.VMEM((NBLK, BLK, BLK), jnp.bfloat16),
            pltpu.VMEM((NBLK, BLK, BLK), jnp.bfloat16),
            pltpu.VMEM((BLK, BLK), jnp.float32),
            pltpu.VMEM((2, NBLK, 1, BLK), jnp.float32),
            pltpu.SemaphoreType.DMA((110,)),
            pltpu.SemaphoreType.DMA((4, 2)),
            pltpu.SemaphoreType.DMA((3, 4, 2)),
            pltpu.SemaphoreType.DMA((2, 3, PARTS)),
            pltpu.SemaphoreType.DMA((PARTS,)),
            pltpu.SemaphoreType.DMA((2, 4)),
            pltpu.SemaphoreType.DMA((2, PARTS)),
            pltpu.SemaphoreType.DMA((2, 15)),
            pltpu.SemaphoreType.DMA((2, 15)),
            pltpu.VMEM((BLK, BLK), jnp.float32),
            pltpu.SMEM((2, 2), jnp.int32),
            pltpu.SemaphoreType.DMA((2,)),
        ],
        compiler_params=pltpu.CompilerParams(
            collective_id=0, has_side_effects=True, vmem_limit_bytes=60 * 2**20
        ),
        cost_estimate=pl.CostEstimate(
            flops=2 * BLK * BLK * BLK * NBLK, bytes_accessed=4 * 2**20, transcendentals=0
        ),
    )(values, tile_mask)
    return scaled * scaled


def solution(mesh):
    return jax.shard_map(
        shards,
        mesh=mesh,
        in_specs=(P("row", "col"), P("row", "col")),
        out_specs=P("row", "col"),
        check_vma=False,
    )
```

```python
import jax
import jax.numpy as jnp
from jax import lax
from jax.experimental import pallas as pl
from jax.experimental.pallas import tpu as pltpu
from jax.sharding import PartitionSpec as P

TILE = 256
BLK = 512
HALF = BLK // 2
PARTS = 4
NBLK = 16
MESH = pl.DeviceIdType.MESH


def kernel(
    values_hbm,
    mask_hbm,
    scaled_ref,
    c_ref,
    a_buf,
    b_buf,
    masked,
    sums,
    send,
    z_recv,
    y_recv,
    x_recv,
    zh_recv,
    core_recv,
    far_recv,
    sum_send,
    sum_recv,
    values_ref,
    mask_ref,
    in_sem,
):
    r = lax.axis_index("row")
    c = lax.axis_index("col")
    y, zl = r // 4, r % 4
    zh, x, core = c // 8, (c // 2) % 4, c % 2
    middle = (zl + 1) // 2 == 1
    near = zl + 1 - 2 * (zl % 2)
    far_side = 3 - zl
    order = [zl, near, 2 - zl // 2, 3 - 3 * (zl // 2)]

    def at_y(d):
        return (((y + d) % 4) * 4 + zl, c)

    def at_zl(z):
        return (y * 4 + z, c)

    def at_x(d):
        return (r, zh * 8 + ((x + d) % 4) * 2 + core)

    across = (r, (c + 8) % 16)
    sibling = (r, c + 1 - 2 * core)

    values_in = pltpu.make_async_copy(values_hbm, values_ref, in_sem.at[0])
    mask_in = pltpu.make_async_copy(mask_hbm, mask_ref, in_sem.at[1])
    values_in.start()
    mask_in.start()

    barrier = pltpu.get_barrier_semaphore()
    shifts = [(dy, dz) for dy in range(4) for dz in range(4) if dy or dz]

    def in_column(dy, dz):
        return (((y + dy) % 4) * 4 + (zl + dz) % 4, c)

    partners = [in_column(dy, dz) for dy, dz in shifts]
    partners += [at_x(1), at_x(3), across, sibling]
    for p in partners:
        pl.semaphore_signal(barrier, inc=1, device_id=p, device_id_type=MESH)

    mask_in.wait()
    values_in.wait()
    for i in range(2):
        for j in range(2):
            rows, cols = pl.ds(i * TILE, TILE), pl.ds(j * TILE, TILE)
            masked[rows, cols] = values_ref[rows, cols] * mask_ref[i, j].astype(jnp.float32)
    sums[0, r] = jnp.sum(masked[...], axis=0, keepdims=True)
    pl.semaphore_wait(barrier, len(partners))

    def sum_copy(base, n, slot):
        return pltpu.make_async_remote_copy(
            src_ref=sums.at[base, slot],
            dst_ref=sums.at[base, slot],
            send_sem=sum_send.at[base, n],
            recv_sem=sum_recv.at[base, n],
            device_id=in_column(*shifts[n]),
            device_id_type=MESH,
        )

    def start_sum(base):
        for n in range(len(shifts)):
            sum_copy(base, n, r).start()

    def finish_sum(base):
        for n, (dy, dz) in enumerate(shifts):
            sum_copy(base, n, ((y + 4 - dy) % 4) * 4 + (zl + 4 - dz) % 4).wait_recv()
        for n in range(len(shifts)):
            sum_copy(base, n, r).wait_send()
        return jnp.sum(sums[base], axis=0)

    start_sum(0)
    c_ref[...] = jnp.zeros_like(c_ref)
    inverse = 1.0 / finish_sum(0)

    def make_stoch(h):
        rows = pl.ds(h * HALF, HALF)
        stoch = (masked[rows] * inverse).astype(jnp.bfloat16)
        b_buf[r, rows] = stoch
        a_buf[c, rows] = stoch


    pending = []
    inner = []

    def piece(buf, k, h):
        if h is None:
            return buf.at[k]
        n = PARTS if buf is a_buf else 2
        return buf.at[k, pl.ds(h * (BLK // n), BLK // n)]


    def push(buf, k, h, sem, dev):
        part = piece(buf, k, h)
        cp = pltpu.make_async_remote_copy(
            src_ref=part,
            dst_ref=part,
            send_sem=send.at[len(pending)],
            recv_sem=sem,
            device_id=dev,
            device_id_type=MESH,
        )
        cp.start()
        pending.append(cp)

    def take(buf, k, h, sem):
        part = piece(buf, k, h)
        pltpu.make_async_remote_copy(
            src_ref=part,
            dst_ref=part,
            send_sem=send.at[0],
            recv_sem=sem,
            device_id=sibling,
            device_id_type=MESH,
        ).wait_recv()

    def b_row(d, q):
        return ((y + d) % 4) * 4 + order[q]

    def a_col(s, d):
        return ((zh + s) % 2) * 8 + ((x + d) % 4) * 2 + core

    def z_start(h):
        push(b_buf, r, h, z_recv.at[zl, h], at_zl(near))
        if inner[-1]:
            push(b_buf, r, h, z_recv.at[zl, h], at_zl(far_side))

    def z_take(q, h):
        o = order[q]
        k = y * 4 + o
        take(b_buf, k, h, z_recv.at[o, h])
        if inner[-1]:
            push(b_buf, k, h, z_recv.at[o, h], at_zl(far_side if q == 1 else near))
        y_start(q, h)

    def y_start(q, h):
        k = b_row(0, q)
        push(b_buf, k, h, y_recv.at[0, q, h], at_y(1))
        push(b_buf, k, h, y_recv.at[1, q, h], at_y(3))

    def y_forward(q, h):
        k = b_row(3 if h == 0 else 1, q)
        take(b_buf, k, h, y_recv.at[h, q, h])
        push(b_buf, k, h, y_recv.at[2, q, h], at_y(1 if h == 0 else 3))

    def x_start(s, h):
        k = a_col(s, 0)
        push(a_buf, k, h, x_recv.at[s, 0, h], at_x(1))
        push(a_buf, k, h, x_recv.at[s, 1, h], at_x(3))

    def x_forward(s, h):
        d = 0 if h < PARTS // 2 else 1
        k = a_col(s, 3 if d == 0 else 1)
        take(a_buf, k, h, x_recv.at[s, d, h])
        push(a_buf, k, h, x_recv.at[s, 2, h], at_x(1 if d == 0 else 3))

    def to_sibling(s, d):
        push(a_buf, a_col(s, d), None, core_recv.at[s, d], sibling)

    def x_share(s):
        for h in range(PARTS // 2, PARTS):
            take(a_buf, a_col(s, 3), h, x_recv.at[s, 0, h])
        to_sibling(s, 3)
        for h in range(PARTS // 2):
            take(a_buf, a_col(s, 1), h, x_recv.at[s, 1, h])
        to_sibling(s, 1)

    def x_share_far(s):
        for h in range(PARTS):
            take(a_buf, a_col(s, 2), h, x_recv.at[s, 2, h])
            push(a_buf, a_col(s, 2), h, far_recv.at[s, h], sibling)

    def across_start(h):
        push(a_buf, c, h, zh_recv.at[h], across)

    def across_take(h):
        take(a_buf, a_col(1, 0), h, zh_recv.at[h])
        x_start(1, h)

    def rest(q):
        take(b_buf, b_row(3, q), 1, y_recv.at[0, q, 1])
        take(b_buf, b_row(1, q), 0, y_recv.at[1, q, 0])
        if q < 3:
            far(q)

    def far(q):
        for h in (0, 1):
            take(b_buf, b_row(2, q), h, y_recv.at[2, q, h])

    def from_sibling(s, d):
        k = ((zh + s) % 2) * 8 + ((x + d) % 4) * 2 + 1 - core
        if d == 2:
            for h in range(PARTS):
                take(a_buf, k, h, far_recv.at[s, h])
        else:
            take(a_buf, k, None, core_recv.at[s, d])

    def product(*ks):
        total = c_ref[...]
        for k in ks:
            total += jnp.dot(a_buf[k], b_buf[k], preferred_element_type=jnp.float32)
        c_ref[...] = total

    def products(q, s):
        k = ((zh + s) % 2) * 8 + order[q]
        product(k, k + 4)

    def a_late(k):
        return (k // 8 != zh) & ((k % 8) // 2 == (x + 2) % 4)

    def sweep_near():
        @pl.loop(0, NBLK // 2)
        def _(i):
            k = ((zh + 1) % 2) * 8 + i

            @pl.when(jnp.logical_not(a_late(k)) & (k % 4 != order[3]))
            def _():
                product(k)

    def sweep_fourth():
        for d in (0, 1, 3):
            k = b_row(d, 3)

            @pl.when(jnp.logical_not(a_late(k)))
            def _():
                product(k)

    def sweep_last():
        k = ((zh + 1) % 2) * 8 + ((x + 2) % 4) * 2
        product(k, k + 1)
        k = b_row(2, 3)

        @pl.when(jnp.logical_not(a_late(k)))
        def _():
            product(k)

    def wait_sent():
        for cp in pending:
            cp.wait_send()

    @pl.when(jnp.logical_not(middle))
    def _():
        inner.append(False)
        pending.clear()
        make_stoch(0)
        z_start(0)
        y_start(0, 0)
        make_stoch(1)
        z_start(1)
        y_start(0, 1)
        x_start(0, 0)
        x_start(0, 1)
        x_start(0, 2)
        x_start(0, 3)
        to_sibling(0, 0)
        z_take(1, 0)
        y_forward(0, 0)
        across_start(0)
        y_forward(0, 1)
        x_forward(0, 0)
        x_forward(0, 1)
        x_forward(0, 2)
        x_forward(0, 3)
        z_take(1, 1)
        across_start(1)
        y_forward(1, 0)
        x_share(0)
        z_take(2, 0)
        across_start(2)
        across_start(3)
        y_forward(1, 1)
        x_share_far(0)
        from_sibling(0, 0)
        from_sibling(0, 3)
        from_sibling(0, 1)
        from_sibling(0, 2)
        rest(0)
        products(0, 0)
        z_take(2, 1)
        across_take(0)
        y_forward(2, 0)
        across_take(1)
        z_take(3, 0)
        across_take(2)
        y_forward(2, 1)
        across_take(3)
        x_forward(1, 0)
        x_forward(1, 1)
        rest(1)
        products(1, 0)
        z_take(3, 1)
        x_forward(1, 2)
        x_forward(1, 3)
        to_sibling(1, 0)
        y_forward(3, 0)
        x_share(1)
        y_forward(3, 1)
        x_share_far(1)
        rest(2)
        products(2, 0)
        from_sibling(1, 0)
        from_sibling(1, 3)
        from_sibling(1, 1)
        sweep_near()
        rest(3)
        sweep_fourth()
        far(3)
        from_sibling(1, 2)
        sweep_last()
        wait_sent()

    @pl.when(middle)
    def _():
        inner.append(True)
        pending.clear()
        make_stoch(0)
        z_start(0)
        y_start(0, 0)
        make_stoch(1)
        z_start(1)
        y_start(0, 1)
        x_start(0, 0)
        x_start(0, 1)
        x_start(0, 2)
        x_start(0, 3)
        to_sibling(0, 0)
        z_take(1, 0)
        z_take(2, 0)
        y_forward(0, 0)
        across_start(0)
        z_take(1, 1)
        z_take(2, 1)
        y_forward(0, 1)
        x_forward(0, 0)
        x_forward(0, 1)
        x_forward(0, 2)
        x_forward(0, 3)
        across_start(1)
        z_take(3, 0)
        y_forward(1, 0)
        x_share(0)
        z_take(3, 1)
        across_start(2)
        across_start(3)
        y_forward(1, 1)
        x_share_far(0)
        from_sibling(0, 0)
        from_sibling(0, 3)
        from_sibling(0, 1)
        from_sibling(0, 2)
        rest(0)
        products(0, 0)
        across_take(0)
        y_forward(2, 0)
        across_take(1)
        across_take(2)
        y_forward(2, 1)
        across_take(3)
        rest(1)
        products(1, 0)
        x_forward(1, 0)
        x_forward(1, 1)
        x_forward(1, 2)
        x_forward(1, 3)
        to_sibling(1, 0)
        y_forward(3, 0)
        x_share(1)
        y_forward(3, 1)
        x_share_far(1)
        rest(2)
        products(2, 0)
        from_sibling(1, 0)
        from_sibling(1, 3)
        from_sibling(1, 1)
        sweep_near()
        rest(3)
        sweep_fourth()
        far(3)
        from_sibling(1, 2)
        sweep_last()
        wait_sent()

    sums[1, r] = jnp.sum(c_ref[...] * c_ref[...], axis=0, keepdims=True)
    start_sum(1)
    scaled_ref[...] = c_ref[...] * jnp.sqrt(jnp.float32(BLK * NBLK) / finish_sum(1))


def shards(values, tile_mask):
    scaled = pl.pallas_call(
        kernel,
        out_shape=jax.ShapeDtypeStruct((BLK, BLK), jnp.float32),
        in_specs=[
            pl.BlockSpec(memory_space=pltpu.HBM),
            pl.BlockSpec(memory_space=pltpu.HBM),
        ],
        out_specs=pl.BlockSpec(memory_space=pltpu.VMEM),
        scratch_shapes=[
            pltpu.VMEM((BLK, BLK), jnp.float32),
            pltpu.VMEM((NBLK, BLK, BLK), jnp.bfloat16),
            pltpu.VMEM((NBLK, BLK, BLK), jnp.bfloat16),
            pltpu.VMEM((BLK, BLK), jnp.float32),
            pltpu.VMEM((2, NBLK, 1, BLK), jnp.float32),
            pltpu.SemaphoreType.DMA((110,)),
            pltpu.SemaphoreType.DMA((4, 2)),
            pltpu.SemaphoreType.DMA((3, 4, 2)),
            pltpu.SemaphoreType.DMA((2, 3, PARTS)),
            pltpu.SemaphoreType.DMA((PARTS,)),
            pltpu.SemaphoreType.DMA((2, 4)),
            pltpu.SemaphoreType.DMA((2, PARTS)),
            pltpu.SemaphoreType.DMA((2, 15)),
            pltpu.SemaphoreType.DMA((2, 15)),
            pltpu.VMEM((BLK, BLK), jnp.float32),
            pltpu.SMEM((2, 2), jnp.int32),
            pltpu.SemaphoreType.DMA((2,)),
        ],
        compiler_params=pltpu.CompilerParams(
            collective_id=0, has_side_effects=True, vmem_limit_bytes=52 * 2**20
        ),
        cost_estimate=pl.CostEstimate(
            flops=2 * BLK * BLK * BLK * NBLK, bytes_accessed=4 * 2**20, transcendentals=0
        ),
    )(values, tile_mask)
    return scaled * scaled


def solution(mesh):
    return jax.shard_map(
        shards,
        mesh=mesh,
        in_specs=(P("row", "col"), P("row", "col")),
        out_specs=P("row", "col"),
        check_vma=False,
    )
```

```python
import jax
import jax.numpy as jnp
from jax import lax
from jax.experimental import pallas as pl
from jax.experimental.pallas import tpu as pltpu
from jax.sharding import PartitionSpec as P

TILE = 256
BLK = 512
HALF = BLK // 2
PARTS = 4
NBLK = 16
MESH = pl.DeviceIdType.MESH


def kernel(
    values_hbm,
    mask_hbm,
    scaled_ref,
    c_ref,
    a_buf,
    b_buf,
    masked,
    sums,
    send,
    z_recv,
    y_recv,
    x_recv,
    zh_recv,
    core_recv,
    far_recv,
    sum_send,
    sum_recv,
    values_ref,
    mask_ref,
    in_sem,
):
    r = lax.axis_index("row")
    c = lax.axis_index("col")
    y, zl = r // 4, r % 4
    zh, x, core = c // 8, (c // 2) % 4, c % 2
    middle = (zl + 1) // 2 == 1
    near = zl + 1 - 2 * (zl % 2)
    far_side = 3 - zl
    order = [zl, near, 2 - zl // 2, 3 - 3 * (zl // 2)]

    def at_y(d):
        return (((y + d) % 4) * 4 + zl, c)

    def at_zl(z):
        return (y * 4 + z, c)

    def at_x(d):
        return (r, zh * 8 + ((x + d) % 4) * 2 + core)

    across = (r, (c + 8) % 16)
    sibling = (r, c + 1 - 2 * core)

    values_in = pltpu.make_async_copy(values_hbm, values_ref, in_sem.at[0])
    mask_in = pltpu.make_async_copy(mask_hbm, mask_ref, in_sem.at[1])
    values_in.start()
    mask_in.start()

    barrier = pltpu.get_barrier_semaphore()
    shifts = [(dy, dz) for dy in range(4) for dz in range(4) if dy or dz]

    def in_column(dy, dz):
        return (((y + dy) % 4) * 4 + (zl + dz) % 4, c)

    partners = [in_column(dy, dz) for dy, dz in shifts]
    partners += [at_x(1), at_x(3), across, sibling]
    for p in partners:
        pl.semaphore_signal(barrier, inc=1, device_id=p, device_id_type=MESH)

    mask_in.wait()
    values_in.wait()
    for i in range(2):
        for j in range(2):
            rows, cols = pl.ds(i * TILE, TILE), pl.ds(j * TILE, TILE)
            masked[rows, cols] = values_ref[rows, cols] * mask_ref[i, j].astype(jnp.float32)
    sums[0, r] = jnp.sum(masked[...], axis=0, keepdims=True)
    pl.semaphore_wait(barrier, len(partners))

    def sum_copy(base, n, slot):
        return pltpu.make_async_remote_copy(
            src_ref=sums.at[base, slot],
            dst_ref=sums.at[base, slot],
            send_sem=sum_send.at[base, n],
            recv_sem=sum_recv.at[base, n],
            device_id=in_column(*shifts[n]),
            device_id_type=MESH,
        )

    def start_sum(base):
        for n in range(len(shifts)):
            sum_copy(base, n, r).start()

    def finish_sum(base):
        for n, (dy, dz) in enumerate(shifts):
            sum_copy(base, n, ((y + 4 - dy) % 4) * 4 + (zl + 4 - dz) % 4).wait_recv()
        return jnp.sum(sums[base], axis=0)

    start_sum(0)
    c_ref[...] = jnp.zeros_like(c_ref)
    inverse = 1.0 / finish_sum(0)

    def make_stoch(h):
        rows = pl.ds(h * HALF, HALF)
        stoch = (masked[rows] * inverse).astype(jnp.bfloat16)
        b_buf[r, rows] = stoch
        a_buf[c, rows] = stoch


    pending = []
    inner = []

    def piece(buf, k, h):
        if h is None:
            return buf.at[k]
        n = PARTS if buf is a_buf else 2
        return buf.at[k, pl.ds(h * (BLK // n), BLK // n)]


    def push(buf, k, h, sem, dev):
        part = piece(buf, k, h)
        cp = pltpu.make_async_remote_copy(
            src_ref=part,
            dst_ref=part,
            send_sem=send.at[len(pending)],
            recv_sem=sem,
            device_id=dev,
            device_id_type=MESH,
        )
        cp.start()
        pending.append(cp)

    def take(buf, k, h, sem):
        part = piece(buf, k, h)
        pltpu.make_async_remote_copy(
            src_ref=part,
            dst_ref=part,
            send_sem=send.at[0],
            recv_sem=sem,
            device_id=sibling,
            device_id_type=MESH,
        ).wait_recv()

    def b_row(d, q):
        return ((y + d) % 4) * 4 + order[q]

    def a_col(s, d):
        return ((zh + s) % 2) * 8 + ((x + d) % 4) * 2 + core

    def z_start(h):
        push(b_buf, r, h, z_recv.at[zl, h], at_zl(near))
        if inner[-1]:
            push(b_buf, r, h, z_recv.at[zl, h], at_zl(far_side))

    def z_take(q, h):
        o = order[q]
        k = y * 4 + o
        take(b_buf, k, h, z_recv.at[o, h])
        if inner[-1]:
            push(b_buf, k, h, z_recv.at[o, h], at_zl(far_side if q == 1 else near))
        y_start(q, h)

    def y_start(q, h):
        k = b_row(0, q)
        push(b_buf, k, h, y_recv.at[0, q, h], at_y(1))
        push(b_buf, k, h, y_recv.at[1, q, h], at_y(3))

    def y_forward(q, h):
        k = b_row(3 if h == 0 else 1, q)
        take(b_buf, k, h, y_recv.at[h, q, h])
        push(b_buf, k, h, y_recv.at[2, q, h], at_y(1 if h == 0 else 3))

    def x_start(s, h):
        k = a_col(s, 0)
        push(a_buf, k, h, x_recv.at[s, 0, h], at_x(1))
        push(a_buf, k, h, x_recv.at[s, 1, h], at_x(3))

    def x_forward(s, h):
        d = 0 if h < PARTS // 2 else 1
        k = a_col(s, 3 if d == 0 else 1)
        take(a_buf, k, h, x_recv.at[s, d, h])
        push(a_buf, k, h, x_recv.at[s, 2, h], at_x(1 if d == 0 else 3))

    def to_sibling(s, d):
        push(a_buf, a_col(s, d), None, core_recv.at[s, d], sibling)

    def x_share(s):
        for h in range(PARTS // 2, PARTS):
            take(a_buf, a_col(s, 3), h, x_recv.at[s, 0, h])
        to_sibling(s, 3)
        for h in range(PARTS // 2):
            take(a_buf, a_col(s, 1), h, x_recv.at[s, 1, h])
        to_sibling(s, 1)

    def x_share_far(s):
        for h in range(PARTS):
            take(a_buf, a_col(s, 2), h, x_recv.at[s, 2, h])
            push(a_buf, a_col(s, 2), h, far_recv.at[s, h], sibling)

    def across_start(h):
        push(a_buf, c, h, zh_recv.at[h], across)

    def across_take(h):
        take(a_buf, a_col(1, 0), h, zh_recv.at[h])
        x_start(1, h)

    def rest(q):
        take(b_buf, b_row(3, q), 1, y_recv.at[0, q, 1])
        take(b_buf, b_row(1, q), 0, y_recv.at[1, q, 0])
        if q < 3:
            far(q)

    def far(q):
        for h in (0, 1):
            take(b_buf, b_row(2, q), h, y_recv.at[2, q, h])

    def from_sibling(s, d):
        k = ((zh + s) % 2) * 8 + ((x + d) % 4) * 2 + 1 - core
        if d == 2:
            for h in range(PARTS):
                take(a_buf, k, h, far_recv.at[s, h])
        else:
            take(a_buf, k, None, core_recv.at[s, d])

    def product(*ks):
        total = c_ref[...]
        for k in ks:
            total += jnp.dot(a_buf[k], b_buf[k], preferred_element_type=jnp.float32)
        c_ref[...] = total

    def products(q, s):
        k = ((zh + s) % 2) * 8 + order[q]
        product(k, k + 4)

    def a_late(k):
        return (k // 8 != zh) & ((k % 8) // 2 == (x + 2) % 4)

    def sweep_near():
        @pl.loop(0, NBLK // 2)
        def _(i):
            k = ((zh + 1) % 2) * 8 + i

            @pl.when(jnp.logical_not(a_late(k)) & (k % 4 != order[3]))
            def _():
                product(k)

    def sweep_fourth():
        for d in (0, 1, 3):
            k = b_row(d, 3)

            @pl.when(jnp.logical_not(a_late(k)))
            def _():
                product(k)

    def sweep_last():
        k = ((zh + 1) % 2) * 8 + ((x + 2) % 4) * 2
        product(k, k + 1)
        k = b_row(2, 3)

        @pl.when(jnp.logical_not(a_late(k)))
        def _():
            product(k)

    def start_totals():
        sums[1, r] = jnp.sum(c_ref[...] * c_ref[...], axis=0, keepdims=True)
        start_sum(1)

    def wait_sent():
        for cp in pending:
            cp.wait_send()

    @pl.when(jnp.logical_not(middle))
    def _():
        inner.append(False)
        pending.clear()
        make_stoch(0)
        z_start(0)
        y_start(0, 0)
        make_stoch(1)
        z_start(1)
        y_start(0, 1)
        x_start(0, 0)
        x_start(0, 1)
        x_start(0, 2)
        x_start(0, 3)
        to_sibling(0, 0)
        z_take(1, 0)
        y_forward(0, 0)
        across_start(0)
        y_forward(0, 1)
        x_forward(0, 0)
        x_forward(0, 1)
        x_forward(0, 2)
        x_forward(0, 3)
        z_take(1, 1)
        across_start(1)
        y_forward(1, 0)
        x_share(0)
        z_take(2, 0)
        across_start(2)
        across_start(3)
        y_forward(1, 1)
        x_share_far(0)
        from_sibling(0, 0)
        from_sibling(0, 3)
        from_sibling(0, 1)
        from_sibling(0, 2)
        rest(0)
        products(0, 0)
        z_take(2, 1)
        across_take(0)
        y_forward(2, 0)
        across_take(1)
        z_take(3, 0)
        across_take(2)
        y_forward(2, 1)
        across_take(3)
        x_forward(1, 0)
        x_forward(1, 1)
        rest(1)
        products(1, 0)
        z_take(3, 1)
        x_forward(1, 2)
        x_forward(1, 3)
        to_sibling(1, 0)
        y_forward(3, 0)
        x_share(1)
        y_forward(3, 1)
        x_share_far(1)
        rest(2)
        products(2, 0)
        from_sibling(1, 0)
        from_sibling(1, 3)
        from_sibling(1, 1)
        sweep_near()
        rest(3)
        sweep_fourth()
        far(3)
        from_sibling(1, 2)
        sweep_last()
        start_totals()
        wait_sent()

    @pl.when(middle)
    def _():
        inner.append(True)
        pending.clear()
        make_stoch(0)
        z_start(0)
        y_start(0, 0)
        make_stoch(1)
        z_start(1)
        y_start(0, 1)
        x_start(0, 0)
        x_start(0, 1)
        x_start(0, 2)
        x_start(0, 3)
        to_sibling(0, 0)
        z_take(1, 0)
        z_take(2, 0)
        y_forward(0, 0)
        across_start(0)
        z_take(1, 1)
        z_take(2, 1)
        y_forward(0, 1)
        x_forward(0, 0)
        x_forward(0, 1)
        x_forward(0, 2)
        x_forward(0, 3)
        across_start(1)
        z_take(3, 0)
        y_forward(1, 0)
        x_share(0)
        z_take(3, 1)
        across_start(2)
        across_start(3)
        y_forward(1, 1)
        x_share_far(0)
        from_sibling(0, 0)
        from_sibling(0, 3)
        from_sibling(0, 1)
        from_sibling(0, 2)
        rest(0)
        products(0, 0)
        across_take(0)
        y_forward(2, 0)
        across_take(1)
        across_take(2)
        y_forward(2, 1)
        across_take(3)
        rest(1)
        products(1, 0)
        x_forward(1, 0)
        x_forward(1, 1)
        x_forward(1, 2)
        x_forward(1, 3)
        to_sibling(1, 0)
        y_forward(3, 0)
        x_share(1)
        y_forward(3, 1)
        x_share_far(1)
        rest(2)
        products(2, 0)
        from_sibling(1, 0)
        from_sibling(1, 3)
        from_sibling(1, 1)
        sweep_near()
        rest(3)
        sweep_fourth()
        far(3)
        from_sibling(1, 2)
        sweep_last()
        start_totals()
        wait_sent()

    scaled_ref[...] = c_ref[...] * jnp.sqrt(jnp.float32(BLK * NBLK) / finish_sum(1))
    for base in (0, 1):
        for n in range(len(shifts)):
            sum_copy(base, n, r).wait_send()


def shards(values, tile_mask):
    scaled = pl.pallas_call(
        kernel,
        out_shape=jax.ShapeDtypeStruct((BLK, BLK), jnp.float32),
        in_specs=[
            pl.BlockSpec(memory_space=pltpu.HBM),
            pl.BlockSpec(memory_space=pltpu.HBM),
        ],
        out_specs=pl.BlockSpec(memory_space=pltpu.VMEM),
        scratch_shapes=[
            pltpu.VMEM((BLK, BLK), jnp.float32),
            pltpu.VMEM((NBLK, BLK, BLK), jnp.bfloat16),
            pltpu.VMEM((NBLK, BLK, BLK), jnp.bfloat16),
            pltpu.VMEM((BLK, BLK), jnp.float32),
            pltpu.VMEM((2, NBLK, 1, BLK), jnp.float32),
            pltpu.SemaphoreType.DMA((110,)),
            pltpu.SemaphoreType.DMA((4, 2)),
            pltpu.SemaphoreType.DMA((3, 4, 2)),
            pltpu.SemaphoreType.DMA((2, 3, PARTS)),
            pltpu.SemaphoreType.DMA((PARTS,)),
            pltpu.SemaphoreType.DMA((2, 4)),
            pltpu.SemaphoreType.DMA((2, PARTS)),
            pltpu.SemaphoreType.DMA((2, 15)),
            pltpu.SemaphoreType.DMA((2, 15)),
            pltpu.VMEM((BLK, BLK), jnp.float32),
            pltpu.SMEM((2, 2), jnp.int32),
            pltpu.SemaphoreType.DMA((2,)),
        ],
        compiler_params=pltpu.CompilerParams(
            collective_id=0, has_side_effects=True, vmem_limit_bytes=52 * 2**20
        ),
        cost_estimate=pl.CostEstimate(
            flops=2 * BLK * BLK * BLK * NBLK, bytes_accessed=4 * 2**20, transcendentals=0
        ),
    )(values, tile_mask)
    return scaled * scaled


def solution(mesh):
    return jax.shard_map(
        shards,
        mesh=mesh,
        in_specs=(P("row", "col"), P("row", "col")),
        out_specs=P("row", "col"),
        check_vma=False,
    )
```

```python
import jax
import jax.numpy as jnp
from jax import lax
from jax.experimental import pallas as pl
from jax.experimental.pallas import tpu as pltpu
from jax.sharding import PartitionSpec as P

TILE = 256
BLK = 512
HALF = BLK // 2
PARTS = 4
NBLK = 16
MESH = pl.DeviceIdType.MESH


def kernel(
    values_hbm,
    mask_hbm,
    scaled_ref,
    c_ref,
    a_buf,
    b_buf,
    masked,
    sums,
    send,
    z_recv,
    y_recv,
    x_recv,
    zh_recv,
    core_recv,
    far_recv,
    sum_send,
    sum_recv,
    values_ref,
    mask_ref,
    in_sem,
):
    r = lax.axis_index("row")
    c = lax.axis_index("col")
    y, zl = r // 4, r % 4
    zh, x, core = c // 8, (c // 2) % 4, c % 2
    middle = (zl + 1) // 2 == 1
    near = zl + 1 - 2 * (zl % 2)
    far_side = 3 - zl
    order = [zl, near, 2 - zl // 2, 3 - 3 * (zl // 2)]

    def at_y(d):
        return (((y + d) % 4) * 4 + zl, c)

    def at_zl(z):
        return (y * 4 + z, c)

    def at_x(d):
        return (r, zh * 8 + ((x + d) % 4) * 2 + core)

    across = (r, (c + 8) % 16)
    sibling = (r, c + 1 - 2 * core)

    values_in = pltpu.make_async_copy(values_hbm, values_ref, in_sem.at[0])
    mask_in = pltpu.make_async_copy(mask_hbm, mask_ref, in_sem.at[1])
    values_in.start()
    mask_in.start()

    barrier = pltpu.get_barrier_semaphore()
    shifts = [(dy, dz) for dy in range(4) for dz in range(4) if dy or dz]

    def in_column(dy, dz):
        return (((y + dy) % 4) * 4 + (zl + dz) % 4, c)

    partners = [in_column(dy, dz) for dy, dz in shifts]
    partners += [at_x(1), at_x(3), across, sibling]
    for p in partners:
        pl.semaphore_signal(barrier, inc=1, device_id=p, device_id_type=MESH)

    mask_in.wait()
    values_in.wait()
    for i in range(2):
        for j in range(2):
            rows, cols = pl.ds(i * TILE, TILE), pl.ds(j * TILE, TILE)
            masked[rows, cols] = values_ref[rows, cols] * mask_ref[i, j].astype(jnp.float32)
    sums[0, r] = jnp.sum(masked[...], axis=0, keepdims=True)
    pl.semaphore_wait(barrier, len(partners))

    def sum_copy(base, n, slot):
        return pltpu.make_async_remote_copy(
            src_ref=sums.at[base, slot],
            dst_ref=sums.at[base, slot],
            send_sem=sum_send.at[base, n],
            recv_sem=sum_recv.at[base, n],
            device_id=in_column(*shifts[n]),
            device_id_type=MESH,
        )

    def start_sum(base):
        for n in range(len(shifts)):
            sum_copy(base, n, r).start()

    def finish_sum(base):
        for n, (dy, dz) in enumerate(shifts):
            sum_copy(base, n, ((y + 4 - dy) % 4) * 4 + (zl + 4 - dz) % 4).wait_recv()
        return jnp.sum(sums[base], axis=0)

    start_sum(0)
    c_ref[...] = jnp.zeros_like(c_ref)
    inverse = 1.0 / finish_sum(0)

    def make_stoch(h):
        rows = pl.ds(h * HALF, HALF)
        stoch = (masked[rows] * inverse).astype(jnp.bfloat16)
        b_buf[r, rows] = stoch
        a_buf[c, rows] = stoch


    pending = []
    inner = []

    def piece(buf, k, h):
        if h is None:
            return buf.at[k]
        n = PARTS if buf is a_buf else 2
        return buf.at[k, pl.ds(h * (BLK // n), BLK // n)]


    def push(buf, k, h, sem, dev):
        part = piece(buf, k, h)
        cp = pltpu.make_async_remote_copy(
            src_ref=part,
            dst_ref=part,
            send_sem=send.at[len(pending)],
            recv_sem=sem,
            device_id=dev,
            device_id_type=MESH,
        )
        cp.start()
        pending.append(cp)

    def take(buf, k, h, sem):
        part = piece(buf, k, h)
        pltpu.make_async_remote_copy(
            src_ref=part,
            dst_ref=part,
            send_sem=send.at[0],
            recv_sem=sem,
            device_id=sibling,
            device_id_type=MESH,
        ).wait_recv()

    def b_row(d, q):
        return ((y + d) % 4) * 4 + order[q]

    def a_col(s, d):
        return ((zh + s) % 2) * 8 + ((x + d) % 4) * 2 + core

    def z_start(h):
        push(b_buf, r, h, z_recv.at[zl, h], at_zl(near))
        if inner[-1]:
            push(b_buf, r, h, z_recv.at[zl, h], at_zl(far_side))

    def z_take(q, h):
        o = order[q]
        k = y * 4 + o
        take(b_buf, k, h, z_recv.at[o, h])
        if inner[-1]:
            push(b_buf, k, h, z_recv.at[o, h], at_zl(far_side if q == 1 else near))
        y_start(q, h)

    def y_start(q, h):
        k = b_row(0, q)
        push(b_buf, k, h, y_recv.at[0, q, h], at_y(1))
        push(b_buf, k, h, y_recv.at[1, q, h], at_y(3))

    def y_forward(q, h):
        k = b_row(3 if h == 0 else 1, q)
        take(b_buf, k, h, y_recv.at[h, q, h])
        push(b_buf, k, h, y_recv.at[2, q, h], at_y(1 if h == 0 else 3))

    def x_start(s, h):
        k = a_col(s, 0)
        push(a_buf, k, h, x_recv.at[s, 0, h], at_x(1))
        push(a_buf, k, h, x_recv.at[s, 1, h], at_x(3))

    def x_forward(s, h):
        d = 0 if h < PARTS // 2 else 1
        k = a_col(s, 3 if d == 0 else 1)
        take(a_buf, k, h, x_recv.at[s, d, h])
        push(a_buf, k, h, x_recv.at[s, 2, h], at_x(1 if d == 0 else 3))

    def to_sibling(s, d):
        push(a_buf, a_col(s, d), None, core_recv.at[s, d], sibling)

    def x_share(s):
        for h in range(PARTS // 2, PARTS):
            take(a_buf, a_col(s, 3), h, x_recv.at[s, 0, h])
        to_sibling(s, 3)
        for h in range(PARTS // 2):
            take(a_buf, a_col(s, 1), h, x_recv.at[s, 1, h])
        to_sibling(s, 1)

    def x_share_far(s):
        for h in range(PARTS):
            take(a_buf, a_col(s, 2), h, x_recv.at[s, 2, h])
            push(a_buf, a_col(s, 2), h, far_recv.at[s, h], sibling)

    def across_start(h):
        push(a_buf, c, h, zh_recv.at[h], across)

    def across_take(h):
        take(a_buf, a_col(1, 0), h, zh_recv.at[h])
        x_start(1, h)

    def rest(q):
        take(b_buf, b_row(3, q), 1, y_recv.at[0, q, 1])
        take(b_buf, b_row(1, q), 0, y_recv.at[1, q, 0])
        if q < 3:
            far(q)

    def far(q):
        for h in (0, 1):
            take(b_buf, b_row(2, q), h, y_recv.at[2, q, h])

    def from_sibling(s, d):
        k = ((zh + s) % 2) * 8 + ((x + d) % 4) * 2 + 1 - core
        if d == 2:
            for h in range(PARTS):
                take(a_buf, k, h, far_recv.at[s, h])
        else:
            take(a_buf, k, None, core_recv.at[s, d])

    def product(*ks):
        total = c_ref[...]
        for k in ks:
            total += jnp.dot(a_buf[k], b_buf[k], preferred_element_type=jnp.float32)
        c_ref[...] = total

    def products(q, s):
        k = ((zh + s) % 2) * 8 + order[q]
        product(k, k + 4)

    def a_late(k):
        return (k // 8 != zh) & ((k % 8) // 2 == (x + 2) % 4)

    def sweep_near():
        @pl.loop(0, NBLK // 2)
        def _(i):
            k = ((zh + 1) % 2) * 8 + i

            @pl.when(jnp.logical_not(a_late(k)) & (k % 4 != order[3]))
            def _():
                product(k)

    def sweep_fourth():
        for d in (0, 1, 3):
            k = b_row(d, 3)

            @pl.when(jnp.logical_not(a_late(k)))
            def _():
                product(k)

    def sweep_last():
        k = ((zh + 1) % 2) * 8 + ((x + 2) % 4) * 2
        product(k, k + 1)
        k = b_row(2, 3)

        @pl.when(jnp.logical_not(a_late(k)))
        def _():
            product(k)

    def start_totals():
        sums[1, r] = jnp.sum(c_ref[...] * c_ref[...], axis=0, keepdims=True)
        start_sum(1)

    def wait_sent():
        for cp in pending:
            cp.wait_send()

    @pl.when(jnp.logical_not(middle))
    def _():
        inner.append(False)
        pending.clear()
        make_stoch(0)
        z_start(0)
        y_start(0, 0)
        make_stoch(1)
        z_start(1)
        y_start(0, 1)
        x_start(0, 0)
        x_start(0, 1)
        x_start(0, 2)
        x_start(0, 3)
        to_sibling(0, 0)
        z_take(1, 0)
        y_forward(0, 0)
        across_start(0)
        y_forward(0, 1)
        x_forward(0, 0)
        x_forward(0, 1)
        x_forward(0, 2)
        x_forward(0, 3)
        z_take(1, 1)
        across_start(1)
        across_start(2)
        y_forward(1, 0)
        x_share(0)
        z_take(2, 0)
        across_start(3)
        y_forward(1, 1)
        x_share_far(0)
        from_sibling(0, 0)
        from_sibling(0, 3)
        from_sibling(0, 1)
        from_sibling(0, 2)
        rest(0)
        products(0, 0)
        z_take(2, 1)
        across_take(0)
        y_forward(2, 0)
        across_take(1)
        z_take(3, 0)
        across_take(2)
        y_forward(2, 1)
        across_take(3)
        x_forward(1, 0)
        x_forward(1, 1)
        rest(1)
        products(1, 0)
        z_take(3, 1)
        x_forward(1, 2)
        x_forward(1, 3)
        to_sibling(1, 0)
        y_forward(3, 0)
        x_share(1)
        y_forward(3, 1)
        x_share_far(1)
        rest(2)
        products(2, 0)
        from_sibling(1, 0)
        from_sibling(1, 3)
        from_sibling(1, 1)
        sweep_near()
        rest(3)
        sweep_fourth()
        far(3)
        from_sibling(1, 2)
        sweep_last()
        start_totals()
        wait_sent()

    @pl.when(middle)
    def _():
        inner.append(True)
        pending.clear()
        make_stoch(0)
        z_start(0)
        y_start(0, 0)
        make_stoch(1)
        z_start(1)
        y_start(0, 1)
        x_start(0, 0)
        x_start(0, 1)
        x_start(0, 2)
        x_start(0, 3)
        to_sibling(0, 0)
        z_take(1, 0)
        z_take(2, 0)
        y_forward(0, 0)
        across_start(0)
        z_take(1, 1)
        z_take(2, 1)
        y_forward(0, 1)
        x_forward(0, 0)
        x_forward(0, 1)
        x_forward(0, 2)
        x_forward(0, 3)
        across_start(1)
        across_start(2)
        z_take(3, 0)
        y_forward(1, 0)
        x_share(0)
        z_take(3, 1)
        across_start(3)
        y_forward(1, 1)
        x_share_far(0)
        from_sibling(0, 0)
        from_sibling(0, 3)
        from_sibling(0, 1)
        from_sibling(0, 2)
        rest(0)
        products(0, 0)
        across_take(0)
        y_forward(2, 0)
        across_take(1)
        across_take(2)
        y_forward(2, 1)
        across_take(3)
        rest(1)
        products(1, 0)
        x_forward(1, 0)
        x_forward(1, 1)
        x_forward(1, 2)
        x_forward(1, 3)
        to_sibling(1, 0)
        y_forward(3, 0)
        x_share(1)
        y_forward(3, 1)
        x_share_far(1)
        rest(2)
        products(2, 0)
        from_sibling(1, 0)
        from_sibling(1, 3)
        from_sibling(1, 1)
        sweep_near()
        rest(3)
        sweep_fourth()
        far(3)
        from_sibling(1, 2)
        sweep_last()
        start_totals()
        wait_sent()

    scaled_ref[...] = c_ref[...] * jnp.sqrt(jnp.float32(BLK * NBLK) / finish_sum(1))
    for base in (0, 1):
        for n in range(len(shifts)):
            sum_copy(base, n, r).wait_send()


def shards(values, tile_mask):
    scaled = pl.pallas_call(
        kernel,
        out_shape=jax.ShapeDtypeStruct((BLK, BLK), jnp.float32),
        in_specs=[
            pl.BlockSpec(memory_space=pltpu.HBM),
            pl.BlockSpec(memory_space=pltpu.HBM),
        ],
        out_specs=pl.BlockSpec(memory_space=pltpu.VMEM),
        scratch_shapes=[
            pltpu.VMEM((BLK, BLK), jnp.float32),
            pltpu.VMEM((NBLK, BLK, BLK), jnp.bfloat16),
            pltpu.VMEM((NBLK, BLK, BLK), jnp.bfloat16),
            pltpu.VMEM((BLK, BLK), jnp.float32),
            pltpu.VMEM((2, NBLK, 1, BLK), jnp.float32),
            pltpu.SemaphoreType.DMA((110,)),
            pltpu.SemaphoreType.DMA((4, 2)),
            pltpu.SemaphoreType.DMA((3, 4, 2)),
            pltpu.SemaphoreType.DMA((2, 3, PARTS)),
            pltpu.SemaphoreType.DMA((PARTS,)),
            pltpu.SemaphoreType.DMA((2, 4)),
            pltpu.SemaphoreType.DMA((2, PARTS)),
            pltpu.SemaphoreType.DMA((2, 15)),
            pltpu.SemaphoreType.DMA((2, 15)),
            pltpu.VMEM((BLK, BLK), jnp.float32),
            pltpu.SMEM((2, 2), jnp.int32),
            pltpu.SemaphoreType.DMA((2,)),
        ],
        compiler_params=pltpu.CompilerParams(
            collective_id=0, has_side_effects=True, vmem_limit_bytes=52 * 2**20
        ),
        cost_estimate=pl.CostEstimate(
            flops=2 * BLK * BLK * BLK * NBLK, bytes_accessed=4 * 2**20, transcendentals=0
        ),
    )(values, tile_mask)
    return scaled * scaled


def solution(mesh):
    return jax.shard_map(
        shards,
        mesh=mesh,
        in_specs=(P("row", "col"), P("row", "col")),
        out_specs=P("row", "col"),
        check_vma=False,
    )
```

```python
import jax
import jax.numpy as jnp
from jax import lax
from jax.experimental import pallas as pl
from jax.experimental.pallas import tpu as pltpu
from jax.sharding import PartitionSpec as P

TILE = 256
BLK = 512
HALF = BLK // 2
PARTS = 4
NBLK = 16
MESH = pl.DeviceIdType.MESH


def kernel(
    values_hbm,
    mask_hbm,
    scaled_ref,
    c_ref,
    a_buf,
    b_buf,
    masked,
    sums,
    send,
    z_recv,
    y_recv,
    x_recv,
    zh_recv,
    core_recv,
    far_recv,
    sum_send,
    sum_recv,
    values_ref,
    mask_ref,
    in_sem,
):
    r = lax.axis_index("row")
    c = lax.axis_index("col")
    y, zl = r // 4, r % 4
    zh, x, core = c // 8, (c // 2) % 4, c % 2
    middle = (zl + 1) // 2 == 1
    near = zl + 1 - 2 * (zl % 2)
    far_side = 3 - zl
    order = [zl, near, 2 - zl // 2, 3 - 3 * (zl // 2)]

    def at_y(d):
        return (((y + d) % 4) * 4 + zl, c)

    def at_zl(z):
        return (y * 4 + z, c)

    def at_x(d):
        return (r, zh * 8 + ((x + d) % 4) * 2 + core)

    across = (r, (c + 8) % 16)
    sibling = (r, c + 1 - 2 * core)

    values_in = [
        pltpu.make_async_copy(
            values_hbm.at[pl.ds(i * HALF, HALF)], values_ref.at[pl.ds(i * HALF, HALF)], in_sem.at[i]
        )
        for i in range(2)
    ]
    mask_in = pltpu.make_async_copy(mask_hbm, mask_ref, in_sem.at[2])
    mask_in.start()
    for cp in values_in:
        cp.start()

    barrier = pltpu.get_barrier_semaphore()
    shifts = [(dy, dz) for dy in range(4) for dz in range(4) if dy or dz]

    def in_column(dy, dz):
        return (((y + dy) % 4) * 4 + (zl + dz) % 4, c)

    partners = [in_column(dy, dz) for dy, dz in shifts]
    partners += [at_x(1), at_x(3), across, sibling]
    for p in partners:
        pl.semaphore_signal(barrier, inc=1, device_id=p, device_id_type=MESH)

    mask_in.wait()
    partial = []
    for i in range(2):
        values_in[i].wait()
        for j in range(2):
            rows, cols = pl.ds(i * TILE, TILE), pl.ds(j * TILE, TILE)
            masked[rows, cols] = values_ref[rows, cols] * mask_ref[i, j].astype(jnp.float32)
        partial.append(jnp.sum(masked[pl.ds(i * HALF, HALF)], axis=0, keepdims=True))
    sums[0, r] = partial[0] + partial[1]
    pl.semaphore_wait(barrier, len(partners))

    def sum_copy(base, n, slot):
        return pltpu.make_async_remote_copy(
            src_ref=sums.at[base, slot],
            dst_ref=sums.at[base, slot],
            send_sem=sum_send.at[base, n],
            recv_sem=sum_recv.at[base, n],
            device_id=in_column(*shifts[n]),
            device_id_type=MESH,
        )

    def start_sum(base):
        for n in range(len(shifts)):
            sum_copy(base, n, r).start()

    def finish_sum(base):
        for n, (dy, dz) in enumerate(shifts):
            sum_copy(base, n, ((y + 4 - dy) % 4) * 4 + (zl + 4 - dz) % 4).wait_recv()
        return jnp.sum(sums[base], axis=0)

    start_sum(0)
    c_ref[...] = jnp.zeros_like(c_ref)
    inverse = 1.0 / finish_sum(0)

    def make_stoch(h):
        rows = pl.ds(h * HALF, HALF)
        stoch = (masked[rows] * inverse).astype(jnp.bfloat16)
        b_buf[r, rows] = stoch
        a_buf[c, rows] = stoch


    pending = []
    inner = []

    def piece(buf, k, h):
        if h is None:
            return buf.at[k]
        n = PARTS if buf is a_buf else 2
        return buf.at[k, pl.ds(h * (BLK // n), BLK // n)]


    def push(buf, k, h, sem, dev):
        part = piece(buf, k, h)
        cp = pltpu.make_async_remote_copy(
            src_ref=part,
            dst_ref=part,
            send_sem=send.at[len(pending)],
            recv_sem=sem,
            device_id=dev,
            device_id_type=MESH,
        )
        cp.start()
        pending.append(cp)

    def take(buf, k, h, sem):
        part = piece(buf, k, h)
        pltpu.make_async_remote_copy(
            src_ref=part,
            dst_ref=part,
            send_sem=send.at[0],
            recv_sem=sem,
            device_id=sibling,
            device_id_type=MESH,
        ).wait_recv()

    def b_row(d, q):
        return ((y + d) % 4) * 4 + order[q]

    def a_col(s, d):
        return ((zh + s) % 2) * 8 + ((x + d) % 4) * 2 + core

    def z_start(h):
        push(b_buf, r, h, z_recv.at[zl, h], at_zl(near))
        if inner[-1]:
            push(b_buf, r, h, z_recv.at[zl, h], at_zl(far_side))

    def z_take(q, h):
        o = order[q]
        k = y * 4 + o
        take(b_buf, k, h, z_recv.at[o, h])
        if inner[-1]:
            push(b_buf, k, h, z_recv.at[o, h], at_zl(far_side if q == 1 else near))
        y_start(q, h)

    def y_start(q, h):
        k = b_row(0, q)
        push(b_buf, k, h, y_recv.at[0, q, h], at_y(1))
        push(b_buf, k, h, y_recv.at[1, q, h], at_y(3))

    def y_forward(q, h):
        k = b_row(3 if h == 0 else 1, q)
        take(b_buf, k, h, y_recv.at[h, q, h])
        push(b_buf, k, h, y_recv.at[2, q, h], at_y(1 if h == 0 else 3))

    def x_start(s, h):
        k = a_col(s, 0)
        push(a_buf, k, h, x_recv.at[s, 0, h], at_x(1))
        push(a_buf, k, h, x_recv.at[s, 1, h], at_x(3))

    def x_forward(s, h):
        d = 0 if h < PARTS // 2 else 1
        k = a_col(s, 3 if d == 0 else 1)
        take(a_buf, k, h, x_recv.at[s, d, h])
        push(a_buf, k, h, x_recv.at[s, 2, h], at_x(1 if d == 0 else 3))

    def to_sibling(s, d):
        push(a_buf, a_col(s, d), None, core_recv.at[s, d], sibling)

    def x_share(s):
        for h in range(PARTS // 2, PARTS):
            take(a_buf, a_col(s, 3), h, x_recv.at[s, 0, h])
        to_sibling(s, 3)
        for h in range(PARTS // 2):
            take(a_buf, a_col(s, 1), h, x_recv.at[s, 1, h])
        to_sibling(s, 1)

    def x_share_far(s):
        for h in range(PARTS):
            take(a_buf, a_col(s, 2), h, x_recv.at[s, 2, h])
            push(a_buf, a_col(s, 2), h, far_recv.at[s, h], sibling)

    def across_start(h):
        push(a_buf, c, h, zh_recv.at[h], across)

    def across_take(h):
        take(a_buf, a_col(1, 0), h, zh_recv.at[h])
        x_start(1, h)

    def rest(q):
        take(b_buf, b_row(3, q), 1, y_recv.at[0, q, 1])
        take(b_buf, b_row(1, q), 0, y_recv.at[1, q, 0])
        if q < 3:
            far(q)

    def far(q):
        for h in (0, 1):
            take(b_buf, b_row(2, q), h, y_recv.at[2, q, h])

    def from_sibling(s, d):
        k = ((zh + s) % 2) * 8 + ((x + d) % 4) * 2 + 1 - core
        if d == 2:
            for h in range(PARTS):
                take(a_buf, k, h, far_recv.at[s, h])
        else:
            take(a_buf, k, None, core_recv.at[s, d])

    def product(*ks):
        total = c_ref[...]
        for k in ks:
            total += jnp.dot(a_buf[k], b_buf[k], preferred_element_type=jnp.float32)
        c_ref[...] = total

    def products(q, s):
        k = ((zh + s) % 2) * 8 + order[q]
        product(k, k + 4)

    def a_late(k):
        return (k // 8 != zh) & ((k % 8) // 2 == (x + 2) % 4)

    def sweep_near():
        @pl.loop(0, NBLK // 2)
        def _(i):
            k = ((zh + 1) % 2) * 8 + i

            @pl.when(jnp.logical_not(a_late(k)) & (k % 4 != order[3]))
            def _():
                product(k)

    def sweep_fourth():
        for d in (0, 1, 3):
            k = b_row(d, 3)

            @pl.when(jnp.logical_not(a_late(k)))
            def _():
                product(k)

    def sweep_last():
        final = b_row(2, 3)
        for i in (0, 1):
            k = ((zh + 1) % 2) * 8 + ((x + 2) % 4) * 2 + i

            @pl.when(k != final)
            def _():
                product(k)

        far(3)
        product(final)

    def start_totals():
        sums[1, r] = jnp.sum(c_ref[...] * c_ref[...], axis=0, keepdims=True)
        start_sum(1)

    def wait_sent():
        for cp in pending:
            cp.wait_send()

    @pl.when(jnp.logical_not(middle))
    def _():
        inner.append(False)
        pending.clear()
        make_stoch(0)
        z_start(0)
        y_start(0, 0)
        make_stoch(1)
        z_start(1)
        y_start(0, 1)
        x_start(0, 0)
        x_start(0, 1)
        x_start(0, 2)
        x_start(0, 3)
        to_sibling(0, 0)
        z_take(1, 0)
        y_forward(0, 0)
        across_start(0)
        y_forward(0, 1)
        x_forward(0, 0)
        x_forward(0, 1)
        x_forward(0, 2)
        x_forward(0, 3)
        z_take(1, 1)
        across_start(1)
        y_forward(1, 0)
        x_share(0)
        z_take(2, 0)
        across_start(2)
        across_start(3)
        y_forward(1, 1)
        x_share_far(0)
        from_sibling(0, 0)
        from_sibling(0, 3)
        from_sibling(0, 1)
        from_sibling(0, 2)
        rest(0)
        products(0, 0)
        z_take(2, 1)
        across_take(0)
        y_forward(2, 0)
        across_take(1)
        z_take(3, 0)
        across_take(2)
        y_forward(2, 1)
        across_take(3)
        x_forward(1, 0)
        x_forward(1, 1)
        rest(1)
        products(1, 0)
        z_take(3, 1)
        x_forward(1, 2)
        x_forward(1, 3)
        to_sibling(1, 0)
        y_forward(3, 0)
        x_share(1)
        y_forward(3, 1)
        x_share_far(1)
        rest(2)
        products(2, 0)
        from_sibling(1, 0)
        from_sibling(1, 3)
        from_sibling(1, 1)
        sweep_near()
        rest(3)
        sweep_fourth()
        from_sibling(1, 2)
        sweep_last()
        start_totals()
        wait_sent()

    @pl.when(middle)
    def _():
        inner.append(True)
        pending.clear()
        make_stoch(0)
        z_start(0)
        y_start(0, 0)
        make_stoch(1)
        z_start(1)
        y_start(0, 1)
        x_start(0, 0)
        x_start(0, 1)
        x_start(0, 2)
        x_start(0, 3)
        to_sibling(0, 0)
        z_take(1, 0)
        z_take(2, 0)
        y_forward(0, 0)
        across_start(0)
        z_take(1, 1)
        z_take(2, 1)
        y_forward(0, 1)
        x_forward(0, 0)
        x_forward(0, 1)
        x_forward(0, 2)
        x_forward(0, 3)
        across_start(1)
        z_take(3, 0)
        y_forward(1, 0)
        x_share(0)
        z_take(3, 1)
        across_start(2)
        across_start(3)
        y_forward(1, 1)
        x_share_far(0)
        from_sibling(0, 0)
        from_sibling(0, 3)
        from_sibling(0, 1)
        from_sibling(0, 2)
        rest(0)
        products(0, 0)
        across_take(0)
        y_forward(2, 0)
        across_take(1)
        across_take(2)
        y_forward(2, 1)
        across_take(3)
        rest(1)
        products(1, 0)
        x_forward(1, 0)
        x_forward(1, 1)
        x_forward(1, 2)
        x_forward(1, 3)
        to_sibling(1, 0)
        y_forward(3, 0)
        x_share(1)
        y_forward(3, 1)
        x_share_far(1)
        rest(2)
        products(2, 0)
        from_sibling(1, 0)
        from_sibling(1, 3)
        from_sibling(1, 1)
        sweep_near()
        rest(3)
        sweep_fourth()
        from_sibling(1, 2)
        sweep_last()
        start_totals()
        wait_sent()

    scaled_ref[...] = c_ref[...] * jnp.sqrt(jnp.float32(BLK * NBLK) / finish_sum(1))
    for base in (0, 1):
        for n in range(len(shifts)):
            sum_copy(base, n, r).wait_send()


def shards(values, tile_mask):
    scaled = pl.pallas_call(
        kernel,
        out_shape=jax.ShapeDtypeStruct((BLK, BLK), jnp.float32),
        in_specs=[
            pl.BlockSpec(memory_space=pltpu.HBM),
            pl.BlockSpec(memory_space=pltpu.HBM),
        ],
        out_specs=pl.BlockSpec(memory_space=pltpu.VMEM),
        scratch_shapes=[
            pltpu.VMEM((BLK, BLK), jnp.float32),
            pltpu.VMEM((NBLK, BLK, BLK), jnp.bfloat16),
            pltpu.VMEM((NBLK, BLK, BLK), jnp.bfloat16),
            pltpu.VMEM((BLK, BLK), jnp.float32),
            pltpu.VMEM((2, NBLK, 1, BLK), jnp.float32),
            pltpu.SemaphoreType.DMA((110,)),
            pltpu.SemaphoreType.DMA((4, 2)),
            pltpu.SemaphoreType.DMA((3, 4, 2)),
            pltpu.SemaphoreType.DMA((2, 3, PARTS)),
            pltpu.SemaphoreType.DMA((PARTS,)),
            pltpu.SemaphoreType.DMA((2, 4)),
            pltpu.SemaphoreType.DMA((2, PARTS)),
            pltpu.SemaphoreType.DMA((2, 15)),
            pltpu.SemaphoreType.DMA((2, 15)),
            pltpu.VMEM((BLK, BLK), jnp.float32),
            pltpu.SMEM((2, 2), jnp.int32),
            pltpu.SemaphoreType.DMA((3,)),
        ],
        compiler_params=pltpu.CompilerParams(
            collective_id=0, has_side_effects=True, vmem_limit_bytes=52 * 2**20
        ),
        cost_estimate=pl.CostEstimate(
            flops=2 * BLK * BLK * BLK * NBLK, bytes_accessed=4 * 2**20, transcendentals=0
        ),
    )(values, tile_mask)
    return scaled * scaled


def solution(mesh):
    return jax.shard_map(
        shards,
        mesh=mesh,
        in_specs=(P("row", "col"), P("row", "col")),
        out_specs=P("row", "col"),
        check_vma=False,
    )
```

```python
import jax
import jax.numpy as jnp
from jax import lax
from jax.experimental import pallas as pl
from jax.experimental.pallas import tpu as pltpu
from jax.sharding import PartitionSpec as P

TILE = 256
BLK = 512
HALF = BLK // 2
PARTS = 4
NBLK = 16
MESH = pl.DeviceIdType.MESH


def kernel(
    values_hbm,
    mask_hbm,
    scaled_ref,
    c_ref,
    a_buf,
    b_buf,
    masked,
    sums,
    send,
    z_recv,
    y_recv,
    x_recv,
    zh_recv,
    core_recv,
    far_recv,
    sum_send,
    sum_recv,
    values_ref,
    mask_ref,
    in_sem,
):
    r = lax.axis_index("row")
    c = lax.axis_index("col")
    y, zl = r // 4, r % 4
    zh, x, core = c // 8, (c // 2) % 4, c % 2
    middle = (zl + 1) // 2 == 1
    near = zl + 1 - 2 * (zl % 2)
    far_side = 3 - zl
    order = [zl, near, 2 - zl // 2, 3 - 3 * (zl // 2)]

    def at_y(d):
        return (((y + d) % 4) * 4 + zl, c)

    def at_zl(z):
        return (y * 4 + z, c)

    def at_x(d):
        return (r, zh * 8 + ((x + d) % 4) * 2 + core)

    across = (r, (c + 8) % 16)
    sibling = (r, c + 1 - 2 * core)

    values_in = [
        pltpu.make_async_copy(
            values_hbm.at[pl.ds(i * HALF, HALF)], values_ref.at[pl.ds(i * HALF, HALF)], in_sem.at[i]
        )
        for i in range(2)
    ]
    mask_in = pltpu.make_async_copy(mask_hbm, mask_ref, in_sem.at[2])
    mask_in.start()
    for cp in values_in:
        cp.start()

    barrier = pltpu.get_barrier_semaphore()
    shifts = [(dy, dz) for dy in (2, 1, 3, 0) for dz in (2, 3, 1, 0) if dy or dz]

    def in_column(dy, dz):
        return (((y + dy) % 4) * 4 + (zl + dz) % 4, c)

    partners = [in_column(dy, dz) for dy, dz in shifts]
    partners += [at_x(1), at_x(3), across, sibling]
    for p in partners:
        pl.semaphore_signal(barrier, inc=1, device_id=p, device_id_type=MESH)

    mask_in.wait()
    partial = []
    for i in range(2):
        values_in[i].wait()
        for j in range(2):
            rows, cols = pl.ds(i * TILE, TILE), pl.ds(j * TILE, TILE)
            masked[rows, cols] = values_ref[rows, cols] * mask_ref[i, j].astype(jnp.float32)
        partial.append(jnp.sum(masked[pl.ds(i * HALF, HALF)], axis=0, keepdims=True))
    sums[0, r] = partial[0] + partial[1]
    pl.semaphore_wait(barrier, len(partners))

    def sum_copy(base, n, slot):
        return pltpu.make_async_remote_copy(
            src_ref=sums.at[base, slot],
            dst_ref=sums.at[base, slot],
            send_sem=sum_send.at[base, n],
            recv_sem=sum_recv.at[base, n],
            device_id=in_column(*shifts[n]),
            device_id_type=MESH,
        )

    def start_sum(base):
        for n in range(len(shifts)):
            sum_copy(base, n, r).start()

    def finish_sum(base):
        for n, (dy, dz) in enumerate(shifts):
            sum_copy(base, n, ((y + 4 - dy) % 4) * 4 + (zl + 4 - dz) % 4).wait_recv()
        return jnp.sum(sums[base], axis=0)

    start_sum(0)
    c_ref[...] = jnp.zeros_like(c_ref)
    inverse = 1.0 / finish_sum(0)

    def make_stoch(h):
        rows = pl.ds(h * HALF, HALF)
        stoch = (masked[rows] * inverse).astype(jnp.bfloat16)
        b_buf[r, rows] = stoch
        a_buf[c, rows] = stoch


    pending = []
    inner = []

    def piece(buf, k, h):
        if h is None:
            return buf.at[k]
        n = PARTS if buf is a_buf else 2
        return buf.at[k, pl.ds(h * (BLK // n), BLK // n)]


    def push(buf, k, h, sem, dev):
        part = piece(buf, k, h)
        cp = pltpu.make_async_remote_copy(
            src_ref=part,
            dst_ref=part,
            send_sem=send.at[len(pending)],
            recv_sem=sem,
            device_id=dev,
            device_id_type=MESH,
        )
        cp.start()
        pending.append(cp)

    def take(buf, k, h, sem):
        part = piece(buf, k, h)
        pltpu.make_async_remote_copy(
            src_ref=part,
            dst_ref=part,
            send_sem=send.at[0],
            recv_sem=sem,
            device_id=sibling,
            device_id_type=MESH,
        ).wait_recv()

    def b_row(d, q):
        return ((y + d) % 4) * 4 + order[q]

    def a_col(s, d):
        return ((zh + s) % 2) * 8 + ((x + d) % 4) * 2 + core

    def z_start(h):
        push(b_buf, r, h, z_recv.at[zl, h], at_zl(near))
        if inner[-1]:
            push(b_buf, r, h, z_recv.at[zl, h], at_zl(far_side))

    def z_take(q, h):
        o = order[q]
        k = y * 4 + o
        take(b_buf, k, h, z_recv.at[o, h])
        if inner[-1]:
            push(b_buf, k, h, z_recv.at[o, h], at_zl(far_side if q == 1 else near))
        y_start(q, h)

    def y_start(q, h):
        k = b_row(0, q)
        push(b_buf, k, h, y_recv.at[0, q, h], at_y(1))
        push(b_buf, k, h, y_recv.at[1, q, h], at_y(3))

    def y_forward(q, h):
        k = b_row(3 if h == 0 else 1, q)
        take(b_buf, k, h, y_recv.at[h, q, h])
        push(b_buf, k, h, y_recv.at[2, q, h], at_y(1 if h == 0 else 3))

    def x_start(s, h):
        k = a_col(s, 0)
        push(a_buf, k, h, x_recv.at[s, 0, h], at_x(1))
        push(a_buf, k, h, x_recv.at[s, 1, h], at_x(3))

    def x_forward(s, h):
        d = 0 if h < PARTS // 2 else 1
        k = a_col(s, 3 if d == 0 else 1)
        take(a_buf, k, h, x_recv.at[s, d, h])
        push(a_buf, k, h, x_recv.at[s, 2, h], at_x(1 if d == 0 else 3))

    def to_sibling(s, d):
        push(a_buf, a_col(s, d), None, core_recv.at[s, d], sibling)

    def x_share(s):
        for h in range(PARTS // 2, PARTS):
            take(a_buf, a_col(s, 3), h, x_recv.at[s, 0, h])
        to_sibling(s, 3)
        for h in range(PARTS // 2):
            take(a_buf, a_col(s, 1), h, x_recv.at[s, 1, h])
        to_sibling(s, 1)

    def x_share_far(s):
        for h in range(PARTS):
            take(a_buf, a_col(s, 2), h, x_recv.at[s, 2, h])
            push(a_buf, a_col(s, 2), h, far_recv.at[s, h], sibling)

    def across_start(h):
        push(a_buf, c, h, zh_recv.at[h], across)

    def across_take(h):
        take(a_buf, a_col(1, 0), h, zh_recv.at[h])
        x_start(1, h)

    def rest(q):
        take(b_buf, b_row(3, q), 1, y_recv.at[0, q, 1])
        take(b_buf, b_row(1, q), 0, y_recv.at[1, q, 0])
        if q < 3:
            far(q)

    def far(q):
        for h in (0, 1):
            take(b_buf, b_row(2, q), h, y_recv.at[2, q, h])

    def from_sibling(s, d):
        k = ((zh + s) % 2) * 8 + ((x + d) % 4) * 2 + 1 - core
        if d == 2:
            for h in range(PARTS):
                take(a_buf, k, h, far_recv.at[s, h])
        else:
            take(a_buf, k, None, core_recv.at[s, d])

    def product(*ks):
        total = c_ref[...]
        for k in ks:
            total += jnp.dot(a_buf[k], b_buf[k], preferred_element_type=jnp.float32)
        c_ref[...] = total

    def products(q, s):
        k = ((zh + s) % 2) * 8 + order[q]
        product(k, k + 4)

    def a_late(k):
        return (k // 8 != zh) & ((k % 8) // 2 == (x + 2) % 4)

    def sweep_near():
        @pl.loop(0, NBLK // 2)
        def _(i):
            k = ((zh + 1) % 2) * 8 + i

            @pl.when(jnp.logical_not(a_late(k)) & (k % 4 != order[3]))
            def _():
                product(k)

    def sweep_fourth():
        for d in (0, 1, 3):
            k = b_row(d, 3)

            @pl.when(jnp.logical_not(a_late(k)))
            def _():
                product(k)

    def sweep_last():
        final = b_row(2, 3)
        for i in (0, 1):
            k = ((zh + 1) % 2) * 8 + ((x + 2) % 4) * 2 + i

            @pl.when(k != final)
            def _():
                product(k)

        far(3)
        product(final)

    def start_totals():
        sums[1, r] = jnp.sum(c_ref[...] * c_ref[...], axis=0, keepdims=True)
        start_sum(1)

    def wait_sent():
        for cp in pending:
            cp.wait_send()

    @pl.when(jnp.logical_not(middle))
    def _():
        inner.append(False)
        pending.clear()
        make_stoch(0)
        z_start(0)
        y_start(0, 0)
        make_stoch(1)
        z_start(1)
        y_start(0, 1)
        x_start(0, 0)
        x_start(0, 1)
        x_start(0, 2)
        x_start(0, 3)
        to_sibling(0, 0)
        z_take(1, 0)
        y_forward(0, 0)
        across_start(0)
        y_forward(0, 1)
        x_forward(0, 0)
        x_forward(0, 1)
        x_forward(0, 2)
        x_forward(0, 3)
        z_take(1, 1)
        across_start(1)
        y_forward(1, 0)
        x_share(0)
        z_take(2, 0)
        across_start(2)
        across_start(3)
        y_forward(1, 1)
        x_share_far(0)
        from_sibling(0, 0)
        from_sibling(0, 3)
        from_sibling(0, 1)
        from_sibling(0, 2)
        rest(0)
        products(0, 0)
        z_take(2, 1)
        across_take(0)
        y_forward(2, 0)
        across_take(1)
        z_take(3, 0)
        across_take(2)
        y_forward(2, 1)
        across_take(3)
        x_forward(1, 0)
        x_forward(1, 1)
        rest(1)
        products(1, 0)
        z_take(3, 1)
        x_forward(1, 2)
        x_forward(1, 3)
        to_sibling(1, 0)
        y_forward(3, 0)
        x_share(1)
        y_forward(3, 1)
        x_share_far(1)
        rest(2)
        products(2, 0)
        from_sibling(1, 0)
        from_sibling(1, 3)
        from_sibling(1, 1)
        sweep_near()
        rest(3)
        sweep_fourth()
        from_sibling(1, 2)
        sweep_last()
        start_totals()
        wait_sent()

    @pl.when(middle)
    def _():
        inner.append(True)
        pending.clear()
        make_stoch(0)
        z_start(0)
        y_start(0, 0)
        make_stoch(1)
        z_start(1)
        y_start(0, 1)
        x_start(0, 0)
        x_start(0, 1)
        x_start(0, 2)
        x_start(0, 3)
        to_sibling(0, 0)
        z_take(1, 0)
        z_take(2, 0)
        y_forward(0, 0)
        across_start(0)
        z_take(1, 1)
        z_take(2, 1)
        y_forward(0, 1)
        x_forward(0, 0)
        x_forward(0, 1)
        x_forward(0, 2)
        x_forward(0, 3)
        across_start(1)
        z_take(3, 0)
        y_forward(1, 0)
        x_share(0)
        z_take(3, 1)
        across_start(2)
        across_start(3)
        y_forward(1, 1)
        x_share_far(0)
        from_sibling(0, 0)
        from_sibling(0, 3)
        from_sibling(0, 1)
        from_sibling(0, 2)
        rest(0)
        products(0, 0)
        across_take(0)
        y_forward(2, 0)
        across_take(1)
        across_take(2)
        y_forward(2, 1)
        across_take(3)
        rest(1)
        products(1, 0)
        x_forward(1, 0)
        x_forward(1, 1)
        x_forward(1, 2)
        x_forward(1, 3)
        to_sibling(1, 0)
        y_forward(3, 0)
        x_share(1)
        y_forward(3, 1)
        x_share_far(1)
        rest(2)
        products(2, 0)
        from_sibling(1, 0)
        from_sibling(1, 3)
        from_sibling(1, 1)
        sweep_near()
        rest(3)
        sweep_fourth()
        from_sibling(1, 2)
        sweep_last()
        start_totals()
        wait_sent()

    scaled_ref[...] = c_ref[...] * jnp.sqrt(jnp.float32(BLK * NBLK) / finish_sum(1))
    for base in (0, 1):
        for n in range(len(shifts)):
            sum_copy(base, n, r).wait_send()


def shards(values, tile_mask):
    scaled = pl.pallas_call(
        kernel,
        out_shape=jax.ShapeDtypeStruct((BLK, BLK), jnp.float32),
        in_specs=[
            pl.BlockSpec(memory_space=pltpu.HBM),
            pl.BlockSpec(memory_space=pltpu.HBM),
        ],
        out_specs=pl.BlockSpec(memory_space=pltpu.VMEM),
        scratch_shapes=[
            pltpu.VMEM((BLK, BLK), jnp.float32),
            pltpu.VMEM((NBLK, BLK, BLK), jnp.bfloat16),
            pltpu.VMEM((NBLK, BLK, BLK), jnp.bfloat16),
            pltpu.VMEM((BLK, BLK), jnp.float32),
            pltpu.VMEM((2, NBLK, 1, BLK), jnp.float32),
            pltpu.SemaphoreType.DMA((110,)),
            pltpu.SemaphoreType.DMA((4, 2)),
            pltpu.SemaphoreType.DMA((3, 4, 2)),
            pltpu.SemaphoreType.DMA((2, 3, PARTS)),
            pltpu.SemaphoreType.DMA((PARTS,)),
            pltpu.SemaphoreType.DMA((2, 4)),
            pltpu.SemaphoreType.DMA((2, PARTS)),
            pltpu.SemaphoreType.DMA((2, 15)),
            pltpu.SemaphoreType.DMA((2, 15)),
            pltpu.VMEM((BLK, BLK), jnp.float32),
            pltpu.SMEM((2, 2), jnp.int32),
            pltpu.SemaphoreType.DMA((3,)),
        ],
        compiler_params=pltpu.CompilerParams(
            collective_id=0, has_side_effects=True, vmem_limit_bytes=52 * 2**20
        ),
        cost_estimate=pl.CostEstimate(
            flops=2 * BLK * BLK * BLK * NBLK, bytes_accessed=4 * 2**20, transcendentals=0
        ),
    )(
        pltpu.with_memory_space_constraint(values, pltpu.HBM),
        pltpu.with_memory_space_constraint(tile_mask, pltpu.HBM),
    )
    return scaled * scaled


def solution(mesh):
    return jax.shard_map(
        shards,
        mesh=mesh,
        in_specs=(P("row", "col"), P("row", "col")),
        out_specs=P("row", "col"),
        check_vma=False,
    )
```

```python
import jax
import jax.numpy as jnp
from jax import lax
from jax.experimental import pallas as pl
from jax.experimental.pallas import tpu as pltpu
from jax.sharding import PartitionSpec as P

TILE = 256
BLK = 512
HALF = BLK // 2
PARTS = 4
NBLK = 16
MESH = pl.DeviceIdType.MESH


def kernel(
    values_hbm,
    mask_hbm,
    scaled_ref,
    c_ref,
    a_buf,
    b_buf,
    masked,
    sums,
    send,
    z_recv,
    y_recv,
    x_recv,
    zh_recv,
    core_recv,
    far_recv,
    sum_send,
    sum_recv,
    values_ref,
    mask_ref,
    in_sem,
):
    r = lax.axis_index("row")
    c = lax.axis_index("col")
    y, zl = r // 4, r % 4
    zh, x, core = c // 8, (c // 2) % 4, c % 2
    middle = (zl + 1) // 2 == 1
    near = zl + 1 - 2 * (zl % 2)
    far_side = 3 - zl
    order = [zl, near, 2 - zl // 2, 3 - 3 * (zl // 2)]

    def at_y(d):
        return (((y + d) % 4) * 4 + zl, c)

    def at_zl(z):
        return (y * 4 + z, c)

    def at_x(d):
        return (r, zh * 8 + ((x + d) % 4) * 2 + core)

    across = (r, (c + 8) % 16)
    sibling = (r, c + 1 - 2 * core)

    values_in = [
        pltpu.make_async_copy(
            values_hbm.at[pl.ds(i * HALF, HALF)], values_ref.at[pl.ds(i * HALF, HALF)], in_sem.at[i]
        )
        for i in range(2)
    ]
    mask_in = pltpu.make_async_copy(mask_hbm, mask_ref, in_sem.at[2])
    mask_in.start()
    for cp in values_in:
        cp.start()

    barrier = pltpu.get_barrier_semaphore()
    shifts = [(dy, dz) for dy in (2, 1, 3, 0) for dz in (2, 3, 1, 0) if dy or dz]

    def in_column(dy, dz):
        return (((y + dy) % 4) * 4 + (zl + dz) % 4, c)

    partners = [in_column(dy, dz) for dy, dz in shifts]
    partners += [at_x(1), at_x(3), across, sibling]
    for p in partners:
        pl.semaphore_signal(barrier, inc=1, device_id=p, device_id_type=MESH)

    mask_in.wait()
    partial = []
    for i in range(2):
        values_in[i].wait()
        for j in range(2):
            rows, cols = pl.ds(i * TILE, TILE), pl.ds(j * TILE, TILE)
            masked[rows, cols] = values_ref[rows, cols] * mask_ref[i, j].astype(jnp.float32)
        partial.append(jnp.sum(masked[pl.ds(i * HALF, HALF)], axis=0, keepdims=True))
    sums[0, r] = partial[0] + partial[1]
    pl.semaphore_wait(barrier, len(partners))

    def sum_copy(base, n, slot):
        return pltpu.make_async_remote_copy(
            src_ref=sums.at[base, slot],
            dst_ref=sums.at[base, slot],
            send_sem=sum_send.at[base, n],
            recv_sem=sum_recv.at[base, n],
            device_id=in_column(*shifts[n]),
            device_id_type=MESH,
        )

    def start_sum(base):
        for n in range(len(shifts)):
            sum_copy(base, n, r).start()

    def finish_sum(base):
        for n, (dy, dz) in enumerate(shifts):
            sum_copy(base, n, ((y + 4 - dy) % 4) * 4 + (zl + 4 - dz) % 4).wait_recv()
        return jnp.sum(sums[base], axis=0)

    start_sum(0)
    c_ref[...] = jnp.zeros_like(c_ref)
    inverse = 1.0 / finish_sum(0)

    def make_stoch(h):
        rows = pl.ds(h * HALF, HALF)
        stoch = (masked[rows] * inverse).astype(jnp.bfloat16)
        b_buf[r, rows] = stoch
        a_buf[c, rows] = stoch


    pending = []
    inner = []

    def piece(buf, k, h):
        if h is None:
            return buf.at[k]
        n = PARTS if buf is a_buf else 2
        return buf.at[k, pl.ds(h * (BLK // n), BLK // n)]


    def push(buf, k, h, sem, dev):
        part = piece(buf, k, h)
        cp = pltpu.make_async_remote_copy(
            src_ref=part,
            dst_ref=part,
            send_sem=send.at[len(pending)],
            recv_sem=sem,
            device_id=dev,
            device_id_type=MESH,
        )
        cp.start()
        pending.append(cp)

    def take(buf, k, h, sem):
        part = piece(buf, k, h)
        pltpu.make_async_remote_copy(
            src_ref=part,
            dst_ref=part,
            send_sem=send.at[0],
            recv_sem=sem,
            device_id=sibling,
            device_id_type=MESH,
        ).wait_recv()

    def b_row(d, q):
        return ((y + d) % 4) * 4 + order[q]

    def a_col(s, d):
        return ((zh + s) % 2) * 8 + ((x + d) % 4) * 2 + core

    def z_start(h):
        push(b_buf, r, h, z_recv.at[zl, h], at_zl(near))
        if inner[-1]:
            push(b_buf, r, h, z_recv.at[zl, h], at_zl(far_side))

    def z_take(q, h):
        o = order[q]
        k = y * 4 + o
        take(b_buf, k, h, z_recv.at[o, h])
        if inner[-1]:
            push(b_buf, k, h, z_recv.at[o, h], at_zl(far_side if q == 1 else near))
        y_start(q, h)

    def y_start(q, h):
        k = b_row(0, q)
        push(b_buf, k, h, y_recv.at[0, q, h], at_y(1))
        push(b_buf, k, h, y_recv.at[1, q, h], at_y(3))

    def y_forward(q, h):
        k = b_row(3 if h == 0 else 1, q)
        take(b_buf, k, h, y_recv.at[h, q, h])
        push(b_buf, k, h, y_recv.at[2, q, h], at_y(1 if h == 0 else 3))

    def x_start(s, h):
        k = a_col(s, 0)
        push(a_buf, k, h, x_recv.at[s, 0, h], at_x(1))
        push(a_buf, k, h, x_recv.at[s, 1, h], at_x(3))

    def x_forward(s, h):
        d = 0 if h < PARTS // 2 else 1
        k = a_col(s, 3 if d == 0 else 1)
        take(a_buf, k, h, x_recv.at[s, d, h])
        push(a_buf, k, h, x_recv.at[s, 2, h], at_x(1 if d == 0 else 3))

    def to_sibling(s, d):
        push(a_buf, a_col(s, d), None, core_recv.at[s, d], sibling)

    def x_share(s):
        for h in range(PARTS // 2, PARTS):
            take(a_buf, a_col(s, 3), h, x_recv.at[s, 0, h])
        to_sibling(s, 3)
        for h in range(PARTS // 2):
            take(a_buf, a_col(s, 1), h, x_recv.at[s, 1, h])
        to_sibling(s, 1)

    def x_share_far(s):
        for h in range(PARTS):
            take(a_buf, a_col(s, 2), h, x_recv.at[s, 2, h])
            push(a_buf, a_col(s, 2), h, far_recv.at[s, h], sibling)

    def across_start(h):
        push(a_buf, c, h, zh_recv.at[h], across)

    def across_take(h):
        take(a_buf, a_col(1, 0), h, zh_recv.at[h])
        x_start(1, h)

    def rest(q):
        take(b_buf, b_row(3, q), 1, y_recv.at[0, q, 1])
        take(b_buf, b_row(1, q), 0, y_recv.at[1, q, 0])
        if q < 3:
            far(q)

    def far(q):
        for h in (0, 1):
            take(b_buf, b_row(2, q), h, y_recv.at[2, q, h])

    def from_sibling(s, d):
        k = ((zh + s) % 2) * 8 + ((x + d) % 4) * 2 + 1 - core
        if d == 2:
            for h in range(PARTS):
                take(a_buf, k, h, far_recv.at[s, h])
        else:
            take(a_buf, k, None, core_recv.at[s, d])

    def product(*ks):
        total = c_ref[...]
        for k in ks:
            total += jnp.dot(a_buf[k], b_buf[k], preferred_element_type=jnp.float32)
        c_ref[...] = total

    def products(q, s):
        k = ((zh + s) % 2) * 8 + order[q]
        product(k, k + 4)

    def a_late(k):
        return (k // 8 != zh) & ((k % 8) // 2 == (x + 2) % 4)

    def sweep_near():
        @pl.loop(0, NBLK // 2)
        def _(i):
            k = ((zh + 1) % 2) * 8 + i

            @pl.when(jnp.logical_not(a_late(k)) & (k % 4 != order[3]))
            def _():
                product(k)

    def sweep_fourth():
        for d in (0, 1, 3):
            k = b_row(d, 3)

            @pl.when(jnp.logical_not(a_late(k)))
            def _():
                product(k)

    def sweep_last():
        final = b_row(2, 3)
        for i in (0, 1):
            k = ((zh + 1) % 2) * 8 + ((x + 2) % 4) * 2 + i

            @pl.when(k != final)
            def _():
                product(k)

        far(3)
        product(final)

    def start_totals():
        sums[1, r] = jnp.sum(c_ref[...] * c_ref[...], axis=0, keepdims=True)
        start_sum(1)

    def wait_sent():
        for cp in pending:
            cp.wait_send()

    @pl.when(jnp.logical_not(middle))
    def _():
        inner.append(False)
        pending.clear()
        make_stoch(0)
        z_start(0)
        y_start(0, 0)
        make_stoch(1)
        z_start(1)
        y_start(0, 1)
        z_take(1, 0)
        y_forward(0, 0)
        across_start(0)
        y_forward(0, 1)
        x_start(0, 0)
        x_start(0, 1)
        x_start(0, 2)
        x_start(0, 3)
        to_sibling(0, 0)
        x_forward(0, 0)
        x_forward(0, 1)
        x_forward(0, 2)
        x_forward(0, 3)
        z_take(1, 1)
        across_start(1)
        y_forward(1, 0)
        x_share(0)
        z_take(2, 0)
        across_start(2)
        across_start(3)
        y_forward(1, 1)
        x_share_far(0)
        from_sibling(0, 0)
        from_sibling(0, 3)
        from_sibling(0, 1)
        from_sibling(0, 2)
        rest(0)
        products(0, 0)
        z_take(2, 1)
        across_take(0)
        y_forward(2, 0)
        across_take(1)
        z_take(3, 0)
        across_take(2)
        y_forward(2, 1)
        across_take(3)
        x_forward(1, 0)
        x_forward(1, 1)
        rest(1)
        products(1, 0)
        z_take(3, 1)
        x_forward(1, 2)
        x_forward(1, 3)
        to_sibling(1, 0)
        y_forward(3, 0)
        x_share(1)
        y_forward(3, 1)
        x_share_far(1)
        rest(2)
        products(2, 0)
        from_sibling(1, 0)
        from_sibling(1, 3)
        from_sibling(1, 1)
        sweep_near()
        rest(3)
        sweep_fourth()
        from_sibling(1, 2)
        sweep_last()
        start_totals()
        wait_sent()

    @pl.when(middle)
    def _():
        inner.append(True)
        pending.clear()
        make_stoch(0)
        z_start(0)
        y_start(0, 0)
        make_stoch(1)
        z_start(1)
        y_start(0, 1)
        z_take(1, 0)
        z_take(2, 0)
        y_forward(0, 0)
        across_start(0)
        z_take(1, 1)
        z_take(2, 1)
        y_forward(0, 1)
        x_start(0, 0)
        x_start(0, 1)
        x_start(0, 2)
        x_start(0, 3)
        to_sibling(0, 0)
        x_forward(0, 0)
        x_forward(0, 1)
        x_forward(0, 2)
        x_forward(0, 3)
        across_start(1)
        z_take(3, 0)
        y_forward(1, 0)
        x_share(0)
        z_take(3, 1)
        across_start(2)
        across_start(3)
        y_forward(1, 1)
        x_share_far(0)
        from_sibling(0, 0)
        from_sibling(0, 3)
        from_sibling(0, 1)
        from_sibling(0, 2)
        rest(0)
        products(0, 0)
        across_take(0)
        y_forward(2, 0)
        across_take(1)
        across_take(2)
        y_forward(2, 1)
        across_take(3)
        rest(1)
        products(1, 0)
        x_forward(1, 0)
        x_forward(1, 1)
        x_forward(1, 2)
        x_forward(1, 3)
        to_sibling(1, 0)
        y_forward(3, 0)
        x_share(1)
        y_forward(3, 1)
        x_share_far(1)
        rest(2)
        products(2, 0)
        from_sibling(1, 0)
        from_sibling(1, 3)
        from_sibling(1, 1)
        sweep_near()
        rest(3)
        sweep_fourth()
        from_sibling(1, 2)
        sweep_last()
        start_totals()
        wait_sent()

    scaled_ref[...] = c_ref[...] * jnp.sqrt(jnp.float32(BLK * NBLK) / finish_sum(1))
    for base in (0, 1):
        for n in range(len(shifts)):
            sum_copy(base, n, r).wait_send()


def shards(values, tile_mask):
    scaled = pl.pallas_call(
        kernel,
        out_shape=jax.ShapeDtypeStruct((BLK, BLK), jnp.float32),
        in_specs=[
            pl.BlockSpec(memory_space=pltpu.HBM),
            pl.BlockSpec(memory_space=pltpu.HBM),
        ],
        out_specs=pl.BlockSpec(memory_space=pltpu.VMEM),
        scratch_shapes=[
            pltpu.VMEM((BLK, BLK), jnp.float32),
            pltpu.VMEM((NBLK, BLK, BLK), jnp.bfloat16),
            pltpu.VMEM((NBLK, BLK, BLK), jnp.bfloat16),
            pltpu.VMEM((BLK, BLK), jnp.float32),
            pltpu.VMEM((2, NBLK, 1, BLK), jnp.float32),
            pltpu.SemaphoreType.DMA((110,)),
            pltpu.SemaphoreType.DMA((4, 2)),
            pltpu.SemaphoreType.DMA((3, 4, 2)),
            pltpu.SemaphoreType.DMA((2, 3, PARTS)),
            pltpu.SemaphoreType.DMA((PARTS,)),
            pltpu.SemaphoreType.DMA((2, 4)),
            pltpu.SemaphoreType.DMA((2, PARTS)),
            pltpu.SemaphoreType.DMA((2, 15)),
            pltpu.SemaphoreType.DMA((2, 15)),
            pltpu.VMEM((BLK, BLK), jnp.float32),
            pltpu.SMEM((2, 2), jnp.int32),
            pltpu.SemaphoreType.DMA((3,)),
        ],
        compiler_params=pltpu.CompilerParams(
            collective_id=0, has_side_effects=True, vmem_limit_bytes=52 * 2**20
        ),
        cost_estimate=pl.CostEstimate(
            flops=2 * BLK * BLK * BLK * NBLK, bytes_accessed=4 * 2**20, transcendentals=0
        ),
    )(
        pltpu.with_memory_space_constraint(values, pltpu.HBM),
        pltpu.with_memory_space_constraint(tile_mask, pltpu.HBM),
    )
    return scaled * scaled


def solution(mesh):
    return jax.shard_map(
        shards,
        mesh=mesh,
        in_specs=(P("row", "col"), P("row", "col")),
        out_specs=P("row", "col"),
        check_vma=False,
    )
```
